32 devices in a mesh: gx: 4 (over y, x), gy: 8 (over z, core).
Axes of the slice: x: 2, y: 2, z: 4, core: 2. Of those that a mesh axis runs over, the one named last changes fastest.
Arguments:
- adjoint: float32 [5, 16, 128, 256], P(None, 'gx', 'gy'), may hold values from -6 to 6
- jac_x: bfloat16 [5, 5, 16, 128, 256], P(None, None, 'gx', 'gy'), may hold values from -2.5 to 2.5
- jac_y: bfloat16 [5, 5, 16, 128, 256], P(None, None, 'gx', 'gy'), may hold values from -2.5 to 2.5
- alpha_x: float32 [16], replicated, may hold values from 0.49375 to 0.498125
- metric_x: float32 [16], P('gx'), may hold values from 0.15 to 0.6
- alpha_y: float32 [128], replicated, may hold values from 0.49960938 to 0.49988282
- metric_y: float32 [128], P('gy'), may hold values from 0.15 to 0.6
- surf_values: float32 [32, 5, 512], P(('gx', 'gy')), may hold values from -12 to 12
- surf_cells: int32 [32, 512], P(('gx', 'gy')), may hold values from 0 to 16383
- surf_owner: int32 [32, 512, 1], P(('gx', 'gy')), may hold values from 0 to 31; in each aligned block of 512 rows (0 to 511, 512 to 1023, ..., all dimensions but the last counted through in order) at most 32 rows name the same one
Outputs:
- adjoint_rhs: float32 [5, 16, 128, 256], P(None, 'gx', 'gy')
The draws below stay inside these ranges and needn't reach their ends.
Inputs may be any that keep to these rules, and one draw needn't show every extreme that they name: `surf_owner`: within the 512 points of one device no owner appears more than 32 times, and some owner appears exactly 32 times.
All inputs are finite; a program needn't handle non-finite values.
Results may differ from the reference program's by a relative error of at most 0.0003.
Values sent between devices are 32-bit elements; how exact they have to be, the bound alone decides.
No kernel may reach another device: no remote copies, remote signals or barrier semaphores. Data moves between devices by JAX's collectives and lax.ppermute only.
A program may use at most 64 MiB of HBM per device.

```python
import math
import jax
import jax.numpy as jnp
import numpy as np
from jax import lax

FIELDS = 5
CX = 4
CY = 16
CZ = 256
SURF = 512
CAP = 32
NX = 16
NY = 128
NZ = 256
N_GY = 8
DEVICES = 32


def plant(values, own_key, smallest, largest):
    extent = values.shape
    place = [jax.random.randint(jax.random.fold_in(own_key, axis), (), 0, extent[axis]) for axis in range(len(extent))]
    values = values.at[tuple(place)].set(smallest)
    longest = extent.index(max(extent))
    place[longest] = (place[longest] + 1) % extent[longest]
    return values.at[tuple(place)].set(largest)


def levels(rng, dims, cuts, smallest, largest):
    def one(dim, shards_of):
        draws = jax.random.uniform(jax.random.fold_in(jax.random.fold_in(rng, 6), dim), (shards_of,), jnp.float32, smallest / len(cuts), largest / len(cuts))
        return jnp.repeat(jnp.exp(draws), dims[dim] // shards_of).reshape((-1,) + (1,) * (len(dims) - dim - 1))

    gain = one(*cuts[0])
    for cut in cuts[1:]:
        gain = gain * one(*cut)
    return gain


def deal_out(stream_key, own, number, rows, number_of, top, most, slope):
    sequence = jax.random.permutation(stream_key, number_of)
    heavy_load, common = load_shares(number_of, rows * top, most, slope, True), load_shares(number_of, rows * top, most, slope, False)
    places = jnp.arange(number_of)

    def named(sizes, turn):
        used = int((sizes > 0).sum())
        fixed = max(1, used // 4)
        moved = fixed + (places - fixed + turn * (used - fixed)) % max(1, number_of - fixed)
        return jnp.zeros((number_of,), jnp.int32).at[sequence[jnp.where(places < fixed, places, moved)]].set(jnp.asarray(sizes, jnp.int32))

    sizes = jnp.where(number % 4 == 0, named(heavy_load, number // 4), named(common, number - number // 4 - 1))
    mixed = jax.random.permutation(jax.random.fold_in(own, 3), number_of)
    donor, taker = mixed[0:number_of // 2 * 2:2], mixed[1:number_of // 2 * 2:2]
    room = jnp.minimum(sizes[donor] - 1, most - sizes[taker]) // 2
    room = jnp.where((donor == sequence[0]) | (taker == sequence[0]) | (sizes[taker] == 0), 0, jnp.maximum(room, 0))
    moved = jax.random.randint(jax.random.fold_in(own, 4), (number_of // 2,), 0, 1 << 20) % (room + 1)
    sizes = sizes.at[donor].add(-moved).at[taker].add(moved)
    labels = jnp.searchsorted(jnp.cumsum(sizes), jnp.arange(rows * top), side="right").astype(jnp.int32)
    table = labels.reshape(top, rows).T
    table = table[jax.random.permutation(jax.random.fold_in(own, 1), rows)]
    turn = jax.random.randint(jax.random.fold_in(own, 2), (rows, 1), 0, top)
    return jnp.take_along_axis(table, (jnp.arange(top)[None, :] + turn) % top, axis=1)


def load_shares(count, total, limit, slope, full):
    weights = [(1 << 20) // math.isqrt(grade ** slope) + 1 for grade in range(1, count + 1)]
    largest = limit if full else min(limit, max(-(-total // count), total * weights[0] // sum(weights)))
    least = 1 if total - largest >= count - 1 else 0
    holding, rest = [largest] + [least] * (count - 1), total - largest - least * (count - 1)
    while rest > 0:
        candidates = [i for i in range(1, count) if holding[i] < largest] or [i for i in range(1, count) if holding[i] < limit]
        mass, remaining = sum([weights[i] for i in candidates]), rest
        for i in candidates:
            extra = min(limit - holding[i], max(1, remaining * weights[i] // mass), rest)
            holding[i] = holding[i] + extra
            rest = rest - extra
    return np.array(holding)


def normal_values(rng, dims, width, most, split=(), held_as=jnp.bfloat16):
    values = jax.random.normal(rng, dims, jnp.float32) * width
    if len(split) > 0:
        values = levels(rng, dims, split, -0.22, 0.18) * values
    return jnp.clip(values, min=-most, max=most).astype(held_as)


def setup_inputs(seed: int = 0) -> dict:
    key_list = jax.random.split(jax.random.key(seed), 11)
    adjoint = normal_values(key_list[0], (FIELDS, NX, NY, NZ), 1.0, 6.0, ((1, 4), (2, 8)), jnp.float32)
    jac_x = normal_values(key_list[1], (FIELDS, FIELDS, NX, NY, NZ), FIELDS ** -0.5, 2.5, ((2, 4), (3, 8)))
    jac_y = normal_values(key_list[2], (FIELDS, FIELDS, NX, NY, NZ), FIELDS ** -0.5, 2.5, ((2, 4), (3, 8)))
    alpha_x = jnp.clip(jax.random.uniform(key_list[3], (NX,), jnp.float32, 0.49375, 0.498125), 0.49375, 0.498125)
    metric_x = jnp.clip(jnp.exp(math.log(0.6) - 1.3862944 * jax.random.uniform(key_list[4], (NX,), jnp.float32) ** levels(key_list[4], (NX,), ((0, 4),), -0.2, 0.2)), 0.15, 0.6)
    alpha_y = jnp.clip(jax.random.uniform(key_list[5], (NY,), jnp.float32, 0.49960938, 0.49988282), 0.49960938, 0.49988282)
    metric_y = jnp.clip(jnp.exp(math.log(0.6) - 1.3862944 * jax.random.uniform(key_list[6], (NY,), jnp.float32) ** levels(key_list[6], (NY,), ((0, 8),), -0.2, 0.2)), 0.15, 0.6)
    surf_values = normal_values(key_list[7], (DEVICES, FIELDS, SURF), 2.0, 12.0, ((0, 32),), jnp.float32)
    surf_cells = plant(jax.random.randint(key_list[8], (DEVICES, SURF), 0, CX * CY * CZ), jax.random.fold_in(key_list[8], 1), 0, (CX * CY * CZ) - 1).astype(jnp.int32)
    surf_owner_keys = jax.random.split(jax.random.fold_in(key_list[9], 1), DEVICES * SURF // SURF)
    surf_owner_turns = jax.random.permutation(jax.random.fold_in(key_list[9], 3), DEVICES * SURF // SURF)
    surf_owner = jax.vmap(lambda own, number: deal_out(jax.random.fold_in(key_list[9], 2), own, number, SURF, DEVICES, 1, CAP, 2))(surf_owner_keys, surf_owner_turns).reshape((DEVICES, SURF, 1))
    return dict(adjoint=adjoint, jac_x=jac_x, jac_y=jac_y, alpha_x=alpha_x, metric_x=metric_x, alpha_y=alpha_y, metric_y=metric_y, surf_values=surf_values, surf_cells=surf_cells, surf_owner=surf_owner)


def shaped(vector, line_axis):
    return vector.reshape((1,) * line_axis + (-1,) + (1,) * (3 - line_axis))


def coefficients(alpha_line):
    lower_diag = alpha_line.at[0].set(0.0)
    upper_diag = alpha_line.at[-1].set(0.0)

    def advance(carried, pieces):
        below_now, above_now = pieces
        pivot_now = 1.0 - below_now * carried
        ratio_now = above_now / pivot_now
        return ratio_now, (pivot_now, ratio_now)

    _, (pivots, ratios) = lax.scan(advance, jnp.zeros((), jnp.float32), (lower_diag, upper_diag))
    return lower_diag, pivots, ratios


def flux_of(jacobian, state_field):
    outputs = []
    for target in range(FIELDS):
        summed = jacobian[0, target].astype(jnp.float32) * state_field[0]
        for source in range(1, FIELDS):
            summed = summed + jacobian[source, target].astype(jnp.float32) * state_field[source]
        outputs.append(summed)
    return jnp.stack(outputs)


def derivative(flux_field, alpha_line, metric_line, line_axis):
    cells_line = flux_field.shape[line_axis]
    widths = [(0, 0)] * 4
    widths[line_axis] = (2, 2)
    padded = jnp.pad(flux_field, widths)
    coef_a = shaped((2.0 / 3.0) * (alpha_line + 2.0), line_axis)
    coef_b = shaped((4.0 * alpha_line - 1.0) / 3.0, line_axis)

    def window(offset):
        return lax.slice_in_dim(padded, offset, offset + cells_line, axis=line_axis)

    right_side = 0.5 * coef_a * (window(3) - window(1)) + 0.25 * coef_b * (window(4) - window(0))
    line_data = jnp.moveaxis(right_side, line_axis, 0)
    lower_diag, pivots, ratios = coefficients(alpha_line)

    def forward(carried, pieces):
        below_now, pivot_now, column = pieces
        result = (column - below_now * carried) / pivot_now
        return result, result

    _, eliminated = lax.scan(forward, jnp.zeros_like(line_data[0]), (lower_diag, pivots, line_data))

    def backward(carried, pieces):
        ratio_now, column = pieces
        result = column - ratio_now * carried
        return result, result

    _, solved = lax.scan(backward, jnp.zeros_like(line_data[0]), (ratios, eliminated), reverse=True)
    slopes = jnp.moveaxis(solved, 0, line_axis)
    return slopes * shaped(metric_line, line_axis)


def reference(adjoint, jac_x, jac_y, alpha_x, metric_x, alpha_y, metric_y, surf_values, surf_cells, surf_owner):
    deriv_x = derivative(flux_of(jac_x, adjoint), alpha_x, metric_x, 1)
    deriv_y = derivative(flux_of(jac_y, adjoint), alpha_y, metric_y, 2)
    owners = surf_owner.reshape(-1)
    cell_ids = surf_cells.reshape(-1)
    payload = jnp.moveaxis(surf_values, 1, 0).reshape(FIELDS, -1)
    grid_x = (owners // N_GY) * CX + cell_ids // (CY * CZ)
    grid_y = (owners % N_GY) * CY + (cell_ids // CZ) % CY
    grid_z = cell_ids % CZ
    forcing = jnp.zeros((FIELDS, NX, NY, NZ), jnp.float32).at[:, grid_x, grid_y, grid_z].add(payload)
    return forcing - (deriv_x + deriv_y)
```

```python
import functools

import jax
import jax.numpy as jnp
from jax import lax
from jax.experimental import pallas as pl
from jax.experimental.pallas import tpu as pltpu
from jax.sharding import PartitionSpec as P

F32 = jnp.float32
BF16 = jnp.bfloat16
NT = (((1,), (1,)), ((), ()))


def moved(row, by, lane, fill):
    lanes = row.shape[1]
    turned = pltpu.roll(row, by % lanes, 1)
    keep = (lane >= by) if by > 0 else (lane < lanes + by)
    return jnp.where(keep, turned, fill)


def running(parts, lane, direction):
    lanes = lane.shape[1]
    a, b, c, d = parts
    step = 1
    while step < lanes:
        shift = step * direction
        a0, b0 = moved(a, shift, lane, 1.0), moved(b, shift, lane, 0.0)
        c0, d0 = moved(c, shift, lane, 0.0), moved(d, shift, lane, 1.0)
        a, b, c, d = a * a0 + b * c0, a * b0 + b * d0, c * a0 + d * c0, c * b0 + d * d0
        step *= 2
    return a + b


def line_rows(alpha, sizes):
    axes, lanes = alpha.shape
    lane = lax.broadcasted_iota(jnp.int32, (axes, lanes), 1)
    which = lax.broadcasted_iota(jnp.int32, (axes, lanes), 0)
    count = jnp.zeros((axes, lanes), jnp.int32)
    for axis, size in enumerate(sizes):
        count = jnp.where(which == axis, size, count)
    inside = lane < count
    alpha = jnp.where(inside, alpha, 0.5)
    slack = 1.0 - 2.0 * alpha
    twice = 2.0 * alpha

    eps = slack + twice * moved(slack, 1, lane, 0.0)
    c = 1.0 - eps
    fwd = running((1.0 + eps, c, eps, c), lane, 1)
    eps = slack + twice * moved(slack, -1, lane, 0.0)
    c = 1.0 - eps
    bwd = running(
        (
            jnp.where(inside, 1.0 + eps, 1.0),
            jnp.where(inside, c, 0.0),
            jnp.where(inside, eps, 0.0),
            jnp.where(inside, c, 1.0),
        ),
        lane,
        -1,
    )
    weight = twice
    step = 1
    while step < lanes:
        weight = weight * moved(weight, step, lane, 1.0)
        step *= 2
    before_w = moved(weight, 1, lane, 1.0)
    before_f = moved(fwd, 1, lane, 1.0)
    after_g = moved(bwd, -1, lane, 1.0)
    whole = jnp.sum(jnp.where(lane == count - 1, fwd, 0.0), axis=1, keepdims=True)
    sign = jnp.where(lane % 2 == 0, 1.0, -1.0)

    p = jnp.where(inside, sign * weight * after_g, 0.0)
    u = jnp.where(inside, sign * before_f / before_w, 0.0)
    q = jnp.where(inside, 2.0 * sign * before_f / (weight * whole), 0.0)
    v = jnp.where(inside, 2.0 * sign * before_w * after_g / whole, 0.0)
    near = (alpha + 2.0) / 3.0
    far = (4.0 * alpha - 1.0) / 12.0

    def folded(row):
        one, two = row * near, row * far
        return (
            moved(one, 1, lane, 0.0)
            - moved(one, -1, lane, 0.0)
            + moved(two, 2, lane, 0.0)
            - moved(two, -2, lane, 0.0)
        )

    diag = p * (moved(q * near, 1, lane, 0.0) + moved(q * far, 2, lane, 0.0)) - u * (
        moved(v * near, -1, lane, 0.0) + moved(v * far, -2, lane, 0.0)
    )
    next_far = moved(jnp.where(inside, far, 0.0), -1, lane, 0.0)
    last_far = moved(far, 1, lane, 0.0)
    low = (p * moved(q, -1, lane, 0.0) - u * moved(v, -1, lane, 0.0)) * next_far
    high = (p * moved(q, 1, lane, 0.0) - u * moved(v, 1, lane, 0.0)) * last_far
    t = jnp.where(inside, folded(q), 0.0)
    s = jnp.where(inside, folded(v), 0.0)
    return [p, u, t, s, diag, low, high]


def packed_points(values, cells, owners, devices, capacity):
    fields, points = values.shape
    owner_of = lax.broadcasted_iota(jnp.int32, (devices, points), 0)
    hot = jnp.where(owner_of == owners, 1.0, 0.0)
    width = 128
    upper = jnp.where(
        lax.broadcasted_iota(jnp.int32, (width, width), 0)
        < lax.broadcasted_iota(jnp.int32, (width, width), 1),
        1.0,
        0.0,
    ).astype(BF16)
    carried = jnp.zeros((devices, 1), F32)
    ranks = []
    for start in range(0, points, width):
        piece = hot[:, start : start + width]
        counts = carried + jnp.dot(piece.astype(BF16), upper, preferred_element_type=F32)
        ranks.append(jnp.sum(piece * counts, axis=0, keepdims=True))
        carried = carried + jnp.sum(piece, axis=1, keepdims=True)
    rank = jnp.concatenate(ranks, axis=1).astype(jnp.int32)
    slot = lax.broadcasted_iota(jnp.int32, (capacity, points), 0) == rank
    rows = [jnp.where(slot, values[f : f + 1], 0.0) for f in range(fields)]
    rows.append(jnp.where(slot, cells.astype(F32), 0.0))
    spread = jnp.concatenate(rows, axis=0)
    top = spread.astype(BF16)
    rest = (spread - top.astype(F32)).astype(BF16)
    hot = hot.astype(BF16)
    return lax.dot_general(hot, top, NT, preferred_element_type=F32) + lax.dot_general(
        hot, rest, NT, preferred_element_type=F32
    )


def first_kernel(
    sizes,
    devices,
    capacity,
    alpha_x,
    alpha_y,
    metric_x,
    metric_y,
    values,
    cells,
    owners,
    adjoint,
    jac_x,
    jac_y,
    pack_out,
    flux_x_out,
    flux_y_out,
    send_x,
    send_y,
    coef_x_out,
    coef_y_out,
    adj,
    jx,
    jy,
    alpha_s,
    sems,
):
    copies = [
        pltpu.make_async_copy(source, target, sems.at[number])
        for number, (source, target) in enumerate(((adjoint, adj), (jac_x, jx), (jac_y, jy)))
    ]
    for copy in copies:
        copy.start()
    fields, cells_x, cells_y, depth = adj.shape
    lanes = alpha_s.shape[1]

    alpha_s[...] = jnp.full(alpha_s.shape, 0.5, F32)
    alpha_s[0:1, 0 : sizes[0]] = alpha_x[...]
    alpha_s[1:2, 0 : sizes[1]] = alpha_y[...]
    rows = line_rows(alpha_s[...], sizes)
    first_x = lax.axis_index("gx") * cells_x
    first_y = lax.axis_index("gy") * cells_y
    coef_x = jnp.concatenate([row[0:1] for row in rows] + [jnp.zeros((1, lanes), F32)], axis=0)
    coef_y = jnp.concatenate([row[1:2] for row in rows] + [jnp.zeros((1, lanes), F32)], axis=0)
    coef_x = pltpu.roll(coef_x, lax.rem(lanes - first_x, lanes), 1)[:, :128]
    coef_y = pltpu.roll(coef_y, lax.rem(lanes - first_y, lanes), 1)[:, :128]
    row_of = lax.broadcasted_iota(jnp.int32, (8, 128), 0)
    scaled = (row_of != 2) & (row_of != 3)
    gain_x = jnp.concatenate([metric_x[...], jnp.zeros((1, 128 - cells_x), F32)], axis=1)
    gain_y = jnp.concatenate([metric_y[...], jnp.zeros((1, 128 - cells_y), F32)], axis=1)
    coef_x = coef_x * jnp.where(scaled, gain_x, 1.0)
    coef_y = coef_y * jnp.where(scaled, gain_y, 1.0)
    coef_x_out[...] = coef_x
    columns_y = jnp.concatenate([coef_y, jnp.zeros((120, 128), F32)], axis=0).T[:cells_y]
    coef_y_out[...] = columns_y

    pack_out[...] = packed_points(values[...], cells[...], owners[...], devices, capacity)

    shape = (cells_y, depth)
    copies[0].wait()
    copies[1].wait()
    totals = [[None, None] for _ in range(fields)]
    for i in range(cells_x):
        state = [adj[k, i] for k in range(fields)]
        for target in range(fields):
            flux = jx[0, target, i].astype(F32) * state[0]
            for k in range(1, fields):
                flux = flux + jx[k, target, i].astype(F32) * state[k]
            flux_x_out[target, i] = flux
            for side in range(2):
                term = jnp.broadcast_to(coef_x[2 + side : 3 + side, i : i + 1], shape) * flux
                if i > 0:
                    term = totals[target][side] + term
                totals[target][side] = term
            if i == 0:
                send_x[2, target] = flux
            if i == cells_x - 1:
                send_x[3, target] = flux
    for target in range(fields):
        for side in range(2):
            send_x[side, target] = totals[target][side]

    weight_t = jnp.broadcast_to(columns_y[:, 2:3], shape)
    weight_s = jnp.broadcast_to(columns_y[:, 3:4], shape)
    copies[2].wait()
    for i in range(cells_x):
        state = [adj[k, i] for k in range(fields)]
        for target in range(fields):
            flux = jy[0, target, i].astype(F32) * state[0]
            for k in range(1, fields):
                flux = flux + jy[k, target, i].astype(F32) * state[k]
            flux_y_out[target, i] = flux
            line = target * cells_x + i
            send_y[0, line : line + 1] = jnp.sum(weight_t * flux, axis=0, keepdims=True)
            send_y[1, line : line + 1] = jnp.sum(weight_s * flux, axis=0, keepdims=True)
            send_y[2, line : line + 1] = flux[0:1]
            send_y[3, line : line + 1] = flux[cells_y - 1 : cells_y]


def flat_slots(received, number, capacity):
    senders = received.shape[0]
    part = received[:, number * capacity : (number + 1) * capacity]
    repeats = 128 // capacity
    tiled = jnp.concatenate([part] * repeats, axis=1)
    lane = lax.broadcasted_iota(jnp.int32, (senders, 128), 1) // capacity
    sender = lax.broadcasted_iota(jnp.int32, (senders, 128), 0)
    rows = []
    for group in range(senders // repeats):
        mine = sender == lane + group * repeats
        rows.append(jnp.sum(jnp.where(mine, tiled, 0.0), axis=0, keepdims=True))
    return jnp.concatenate(rows, axis=1)


def middle_kernel(capacity, received, flux_x, flux_y, coef_x_ref, coef_y_ref, out):
    fields, cells_x, cells_y, depth = out.shape
    rows_block = cells_x * cells_y
    shape = (cells_y, depth)
    got = received[...]
    slots = got.shape[0] * capacity
    flat = [flat_slots(got, f, capacity) for f in range(fields + 1)]
    cell = flat[fields].astype(jnp.int32)
    row_hot = lax.broadcasted_iota(jnp.int32, (rows_block, slots), 0) == cell // depth
    depth_hot = jnp.where(
        lax.broadcasted_iota(jnp.int32, (depth, slots), 0) == cell % depth, 1.0, 0.0
    ).astype(BF16)
    for f in range(fields):
        spread = jnp.where(row_hot, flat[f], 0.0)
        top = spread.astype(BF16)
        rest = (spread - top.astype(F32)).astype(BF16)
        both = lax.dot_general(
            jnp.concatenate([top, rest], axis=0), depth_hot, NT, preferred_element_type=F32
        )
        forcing = both[:rows_block] + both[rows_block:]
        for i in range(cells_x):
            out[f, i] = forcing[i * cells_y : (i + 1) * cells_y]

    coef_x = coef_x_ref[...]
    coef_y = coef_y_ref[...]

    def at_x(row, i):
        return jnp.broadcast_to(coef_x[row : row + 1, i : i + 1], shape)

    wide = [jnp.broadcast_to(coef_y[:, row : row + 1], shape) for row in range(7)]
    station = lax.broadcasted_iota(jnp.int32, shape, 0)

    for f in range(fields):
        stations = [flux_x[f, i] for i in range(cells_x)]
        before = [None] * cells_x
        after = [None] * cells_x
        for i in range(1, cells_x):
            term = at_x(2, i - 1) * stations[i - 1]
            before[i] = term if i == 1 else before[i - 1] + term
        for i in range(cells_x - 2, -1, -1):
            term = at_x(3, i + 1) * stations[i + 1]
            after[i] = term if i == cells_x - 2 else after[i + 1] + term
        for i in range(cells_x):
            total = at_x(4, i) * stations[i]
            if i > 0:
                total = total + at_x(0, i) * before[i] + at_x(5, i) * stations[i - 1]
            if i < cells_x - 1:
                total = total + at_x(1, i) * after[i] + at_x(6, i) * stations[i + 1]

            line = flux_y[f, i]
            below = wide[2] * line
            above = wide[3] * line
            low = jnp.where(station >= 1, pltpu.roll(line, 1, 0), 0.0)
            high = jnp.where(station < cells_y - 1, pltpu.roll(line, cells_y - 1, 0), 0.0)
            below = jnp.where(station >= 1, pltpu.roll(below, 1, 0), 0.0)
            above = jnp.where(station < cells_y - 1, pltpu.roll(above, cells_y - 1, 0), 0.0)
            step = 1
            while step < cells_y:
                below = below + jnp.where(station >= step, pltpu.roll(below, step, 0), 0.0)
                above = above + jnp.where(
                    station < cells_y - step, pltpu.roll(above, cells_y - step, 0), 0.0
                )
                step *= 2
            total = total + wide[0] * below + wide[1] * above
            total = total + wide[4] * line + wide[5] * low + wide[6] * high
            out[f, i] = out[f, i] - total


def last_kernel(base, ends_x, ends_y, coef_x_ref, coef_y_ref, out):
    fields, cells_x, cells_y, depth = out.shape
    shape = (cells_y, depth)
    coef_x = coef_x_ref[...]
    coef_y = coef_y_ref[...]

    def at_x(row, i):
        return jnp.broadcast_to(coef_x[row : row + 1, i : i + 1], shape)

    p_y = jnp.broadcast_to(coef_y[:, 0:1], shape)
    u_y = jnp.broadcast_to(coef_y[:, 1:2], shape)
    station = lax.broadcasted_iota(jnp.int32, shape, 0)
    low_y = jnp.where(station == 0, jnp.broadcast_to(coef_y[:, 5:6], shape), 0.0)
    high_y = jnp.where(station == cells_y - 1, jnp.broadcast_to(coef_y[:, 6:7], shape), 0.0)
    for i in range(cells_x):
        p_x, u_x = at_x(0, i), at_x(1, i)
        for f in range(fields):
            total = p_x * ends_x[0, f] + u_x * ends_x[1, f]
            if i == 0:
                total = total + at_x(5, i) * ends_x[2, f]
            if i == cells_x - 1:
                total = total + at_x(6, i) * ends_x[3, f]
            line = f * cells_x + i
            entering = ends_y[0, line : line + 1]
            leaving = ends_y[1, line : line + 1]
            left = ends_y[2, line : line + 1]
            right = ends_y[3, line : line + 1]
            total = total + p_y * entering + u_y * leaving + low_y * left + high_y * right
            out[f, i] = base[f, i] - total


def swept(own, axis, mirrored):
    count = lax.axis_size(axis)
    place = lax.axis_index(axis)
    zero = jnp.zeros_like(own[0])
    below, above, left, right = zero, zero, zero, zero
    sum_t, sum_u, first, last = own[0], own[1], own[2], own[3]
    bits = max(1, count.bit_length() - 1)
    for bit in range(bits):
        size = 1 << bit
        turn = 2 * size - 1 if mirrored else size
        pairs = [(i, i ^ turn) for i in range(count)]
        upper = (place // size) % 2 == 1
        inner = place % size
        if bit == bits - 1:
            sent = jnp.stack([jnp.where(upper, sum_u, sum_t), jnp.where(upper, first, last)])
            got = lax.ppermute(sent, axis, pairs)
            got_t = got_u = got[0]
            got_first = got_last = got[1]
        elif mirrored:
            sent = jnp.stack([sum_t, sum_u, jnp.where(upper, first, last)])
            got = lax.ppermute(sent, axis, pairs)
            got_t, got_u = got[0], got[1]
            got_first = got_last = got[2]
        else:
            got = lax.ppermute(jnp.stack([sum_t, sum_u, first, last]), axis, pairs)
            got_t, got_u, got_first, got_last = got[0], got[1], got[2], got[3]
        below = jnp.where(upper, below + got_t, below)
        above = jnp.where(upper, above, above + got_u)
        left = jnp.where(upper & (inner == 0), got_last, left)
        right = jnp.where(jnp.logical_not(upper) & (inner == size - 1), got_first, right)
        if bit < bits - 1:
            sum_t, sum_u = sum_t + got_t, sum_u + got_u
            if not mirrored:
                first, last = jnp.where(upper, got_first, first), jnp.where(upper, last, got_last)
    return jnp.stack([below, above, left, right])


def on_device(
    adjoint, jac_x, jac_y, alpha_x, metric_x, alpha_y, metric_y, surf_values, surf_cells, surf_owner
):
    fields, cells_x, cells_y, depth = adjoint.shape
    points = surf_values.shape[2]
    devices = lax.axis_size("gx") * lax.axis_size("gy")
    capacity = max(4, 2 * points // devices)
    sizes = (alpha_x.shape[0], alpha_y.shape[0])
    lanes = -(-max(sizes) // 128) * 128
    vmem = pl.BlockSpec(memory_space=pltpu.VMEM)
    far = pl.BlockSpec(memory_space=pl.ANY)

    def array(*shape):
        return jax.ShapeDtypeStruct(shape, F32)

    pack, flux_x, flux_y, own_x, own_y, coef_x, coef_y = pl.pallas_call(
        functools.partial(first_kernel, sizes, devices, capacity),
        in_specs=[vmem] * 7 + [far] * 3,
        out_specs=[vmem] * 7,
        out_shape=[
            array(devices, (fields + 1) * capacity),
            array(*adjoint.shape),
            array(*adjoint.shape),
            array(4, fields, cells_y, depth),
            array(4, fields * cells_x, depth),
            array(8, 128),
            array(cells_y, 128),
        ],
        scratch_shapes=[
            pltpu.VMEM(adjoint.shape, F32),
            pltpu.VMEM(jac_x.shape, BF16),
            pltpu.VMEM(jac_y.shape, BF16),
            pltpu.VMEM((8, lanes), F32),
            pltpu.SemaphoreType.DMA((3,)),
        ],
        compiler_params=pltpu.CompilerParams(vmem_limit_bytes=24 << 20),
        name="flux_and_sums",
    )(
        alpha_x.reshape(1, -1),
        alpha_y.reshape(1, -1),
        metric_x.reshape(1, -1),
        metric_y.reshape(1, -1),
        surf_values[0],
        surf_cells,
        surf_owner.reshape(1, points),
        adjoint,
        jac_x,
        jac_y,
    )
    received = lax.all_to_all(pack, ("gx", "gy"), 0, 0, tiled=True)
    ends_x = swept(own_x, "gx", True)
    ends_y = swept(own_y, "gy", False)
    base = pl.pallas_call(
        functools.partial(middle_kernel, capacity),
        in_specs=[vmem] * 5,
        out_specs=vmem,
        out_shape=array(*adjoint.shape),
        compiler_params=pltpu.CompilerParams(vmem_limit_bytes=24 << 20),
        name="forcing_and_block_part",
    )(received, flux_x, flux_y, coef_x, coef_y)
    return pl.pallas_call(
        last_kernel,
        in_specs=[vmem] * 5,
        out_specs=vmem,
        out_shape=array(*adjoint.shape),
        compiler_params=pltpu.CompilerParams(vmem_limit_bytes=24 << 20),
        name="far_part",
    )(base, ends_x, ends_y, coef_x, coef_y)


def solution(mesh):
    in_specs = (
        P(None, "gx", "gy", None),
        P(None, None, "gx", "gy", None),
        P(None, None, "gx", "gy", None),
        P(),
        P("gx"),
        P(),
        P("gy"),
        P(("gx", "gy"), None, None),
        P(("gx", "gy"), None),
        P(("gx", "gy"), None, None),
    )
    out_specs = P(None, "gx", "gy", None)
    return jax.shard_map(
        on_device, mesh=mesh, in_specs=in_specs, out_specs=out_specs, check_vma=False
    )
```

```python
import functools

import jax
import jax.numpy as jnp
from jax import lax
from jax.experimental import pallas as pl
from jax.experimental.pallas import tpu as pltpu
from jax.sharding import PartitionSpec as P

F32 = jnp.float32
BF16 = jnp.bfloat16
NT = (((1,), (1,)), ((), ()))


def moved(row, by, lane, fill):
    lanes = row.shape[1]
    turned = pltpu.roll(row, by % lanes, 1)
    keep = (lane >= by) if by > 0 else (lane < lanes + by)
    return jnp.where(keep, turned, fill)


def running(parts, lane, direction):
    lanes = lane.shape[1]
    a, b, c, d = parts
    step = 1
    while step < lanes:
        shift = step * direction
        a0, b0 = moved(a, shift, lane, 1.0), moved(b, shift, lane, 0.0)
        c0, d0 = moved(c, shift, lane, 0.0), moved(d, shift, lane, 1.0)
        a, b, c, d = a * a0 + b * c0, a * b0 + b * d0, c * a0 + d * c0, c * b0 + d * d0
        step *= 2
    return a + b


def line_rows(alpha, sizes):
    axes, lanes = alpha.shape
    lane = lax.broadcasted_iota(jnp.int32, (axes, lanes), 1)
    which = lax.broadcasted_iota(jnp.int32, (axes, lanes), 0)
    count = jnp.zeros((axes, lanes), jnp.int32)
    for axis, size in enumerate(sizes):
        count = jnp.where(which == axis, size, count)
    inside = lane < count
    alpha = jnp.where(inside, alpha, 0.5)
    slack = 1.0 - 2.0 * alpha
    twice = 2.0 * alpha

    eps = slack + twice * moved(slack, 1, lane, 0.0)
    c = 1.0 - eps
    fwd = running((1.0 + eps, c, eps, c), lane, 1)
    eps = slack + twice * moved(slack, -1, lane, 0.0)
    c = 1.0 - eps
    bwd = running(
        (
            jnp.where(inside, 1.0 + eps, 1.0),
            jnp.where(inside, c, 0.0),
            jnp.where(inside, eps, 0.0),
            jnp.where(inside, c, 1.0),
        ),
        lane,
        -1,
    )
    weight = twice
    step = 1
    while step < lanes:
        weight = weight * moved(weight, step, lane, 1.0)
        step *= 2
    before_w = moved(weight, 1, lane, 1.0)
    before_f = moved(fwd, 1, lane, 1.0)
    after_g = moved(bwd, -1, lane, 1.0)
    whole = jnp.sum(jnp.where(lane == count - 1, fwd, 0.0), axis=1, keepdims=True)
    sign = jnp.where(lane % 2 == 0, 1.0, -1.0)

    p = jnp.where(inside, sign * weight * after_g, 0.0)
    u = jnp.where(inside, sign * before_f / before_w, 0.0)
    q = jnp.where(inside, 2.0 * sign * before_f / (weight * whole), 0.0)
    v = jnp.where(inside, 2.0 * sign * before_w * after_g / whole, 0.0)
    near = (alpha + 2.0) / 3.0
    far = (4.0 * alpha - 1.0) / 12.0

    def folded(row):
        one, two = row * near, row * far
        return (
            moved(one, 1, lane, 0.0)
            - moved(one, -1, lane, 0.0)
            + moved(two, 2, lane, 0.0)
            - moved(two, -2, lane, 0.0)
        )

    diag = p * (moved(q * near, 1, lane, 0.0) + moved(q * far, 2, lane, 0.0)) - u * (
        moved(v * near, -1, lane, 0.0) + moved(v * far, -2, lane, 0.0)
    )
    next_far = moved(jnp.where(inside, far, 0.0), -1, lane, 0.0)
    last_far = moved(far, 1, lane, 0.0)
    low = (p * moved(q, -1, lane, 0.0) - u * moved(v, -1, lane, 0.0)) * next_far
    high = (p * moved(q, 1, lane, 0.0) - u * moved(v, 1, lane, 0.0)) * last_far
    t = jnp.where(inside, folded(q), 0.0)
    s = jnp.where(inside, folded(v), 0.0)
    return [p, u, t, s, diag, low, high]


def packed_points(values, cells, owners, devices, capacity):
    points = owners.shape[1]
    owner_of = lax.broadcasted_iota(jnp.int32, (devices, points), 0)
    hot = jnp.where(owner_of == owners, 1.0, 0.0)
    width = 128
    upper = jnp.where(
        lax.broadcasted_iota(jnp.int32, (width, width), 0)
        < lax.broadcasted_iota(jnp.int32, (width, width), 1),
        1.0,
        0.0,
    ).astype(BF16)
    carried = jnp.zeros((devices, 1), F32)
    ranks = []
    for start in range(0, points, width):
        piece = hot[:, start : start + width]
        counts = carried + jnp.dot(piece.astype(BF16), upper, preferred_element_type=F32)
        ranks.append(jnp.sum(piece * counts, axis=0, keepdims=True))
        carried = carried + jnp.sum(piece, axis=1, keepdims=True)
    rank = jnp.concatenate(ranks, axis=1).astype(jnp.int32)
    slot = lax.broadcasted_iota(jnp.int32, (capacity, points), 0) == rank
    rows = [jnp.where(slot, row, 0.0) for row in values]
    rows.append(jnp.where(slot, cells.astype(F32), 0.0))
    spread = jnp.concatenate(rows, axis=0)
    top = spread.astype(BF16)
    rest = (spread - top.astype(F32)).astype(BF16)
    hot = hot.astype(BF16)
    spare = -spread.shape[0] % 128
    if spare:
        top = jnp.concatenate([top, jnp.zeros((spare, points), BF16)], axis=0)
        rest = jnp.concatenate([rest, jnp.zeros((spare, points), BF16)], axis=0)
    return lax.dot_general(hot, top, NT, preferred_element_type=F32) + lax.dot_general(
        hot, rest, NT, preferred_element_type=F32
    )


def fetch(sources, targets, sems):
    copies = [
        pltpu.make_async_copy(source, target, sems.at[number])
        for number, (source, target) in enumerate(zip(sources, targets))
    ]
    for copy in copies:
        copy.start()
    return copies


def points_kernel(sizes, devices, capacity, *refs):
    sources, refs = refs[:7], refs[7:]
    pack, coef_x_out, coef_y_out = refs[:3]
    targets, alpha_s, sems = refs[3:10], refs[10], refs[11]
    alpha_x, alpha_y, metric_x, metric_y, values, cells, owners = targets
    for copy in fetch(sources, targets, sems):
        copy.wait()
    fields = values.shape[0]
    packed = packed_points(
        [values[f] for f in range(fields)], cells[...], owners[...], devices, capacity
    )
    for device in range(devices):
        pack[device] = packed[device : device + 1]

    lanes = alpha_s.shape[1]
    cells_x, cells_y = metric_x.shape[1], metric_y.shape[1]
    alpha_s[...] = jnp.full(alpha_s.shape, 0.5, F32)
    alpha_s[0:1, 0 : sizes[0]] = alpha_x[...]
    alpha_s[1:2, 0 : sizes[1]] = alpha_y[...]
    rows = line_rows(alpha_s[...], sizes)
    first_x = lax.axis_index("gx") * cells_x
    first_y = lax.axis_index("gy") * cells_y
    coef_x = jnp.concatenate([row[0:1] for row in rows] + [jnp.zeros((1, lanes), F32)], axis=0)
    coef_y = jnp.concatenate([row[1:2] for row in rows] + [jnp.zeros((1, lanes), F32)], axis=0)
    coef_x = pltpu.roll(coef_x, lax.rem(lanes - first_x, lanes), 1)[:, :128]
    coef_y = pltpu.roll(coef_y, lax.rem(lanes - first_y, lanes), 1)[:, :128]
    row_of = lax.broadcasted_iota(jnp.int32, (8, 128), 0)
    scaled = (row_of != 2) & (row_of != 3)
    gain_x = jnp.concatenate([metric_x[...], jnp.zeros((1, 128 - cells_x), F32)], axis=1)
    gain_y = jnp.concatenate([metric_y[...], jnp.zeros((1, 128 - cells_y), F32)], axis=1)
    coef_x = coef_x * jnp.where(scaled, gain_x, 1.0)
    coef_y = coef_y * jnp.where(scaled, gain_y, 1.0)
    coef_x_out[...] = coef_x
    coef_y_out[...] = jnp.concatenate([coef_y, jnp.zeros((120, 128), F32)], axis=0).T[:cells_y]


def flux_kernel(coef_x_ref, coef_y_ref, adjoint, jac_x, jac_y, *refs):
    flux_x_out, flux_y_out, send_y = refs[:3]
    faces, targets, sems = refs[3:-4], refs[-4:-1], refs[-1]
    adj, jx, jy = targets
    copies = fetch((adjoint, jac_x, jac_y), targets, sems)
    fields, cells_x, cells_y, depth = adj.shape
    coef_x = coef_x_ref[...]
    columns_y = coef_y_ref[...]
    lines = fields * cells_x
    shape = (cells_y, depth)
    copies[0].wait()
    copies[1].wait()
    totals = [[None, None] for _ in range(fields)]
    for i in range(cells_x):
        state = [adj[k, i] for k in range(fields)]
        for target in range(fields):
            flux = jx[0, target, i].astype(F32) * state[0]
            for k in range(1, fields):
                flux = flux + jx[k, target, i].astype(F32) * state[k]
            flux_x_out[target, i] = flux
            for side in range(2):
                term = jnp.broadcast_to(coef_x[2 + side : 3 + side, i : i + 1], shape) * flux
                if i > 0:
                    term = totals[target][side] + term
                totals[target][side] = term
    for bit, face in enumerate(faces):
        upper = (lax.axis_index("gx") // (1 << bit)) % 2 == 1

        @pl.when(upper)
        def _(face=face):
            for target in range(fields):
                face[0, target] = totals[target][1]
                face[1, target] = flux_x_out[target, 0]

        @pl.when(jnp.logical_not(upper))
        def _(face=face):
            for target in range(fields):
                face[0, target] = totals[target][0]
                face[1, target] = flux_x_out[target, cells_x - 1]

    weight_t = jnp.broadcast_to(columns_y[:, 2:3], shape)
    weight_s = jnp.broadcast_to(columns_y[:, 3:4], shape)
    copies[2].wait()
    for i in range(cells_x):
        state = [adj[k, i] for k in range(fields)]
        for target in range(fields):
            flux = jy[0, target, i].astype(F32) * state[0]
            for k in range(1, fields):
                flux = flux + jy[k, target, i].astype(F32) * state[k]
            flux_y_out[target, i] = flux
            line = target * cells_x + i
            rows = (
                jnp.sum(weight_t * flux, axis=0, keepdims=True),
                jnp.sum(weight_s * flux, axis=0, keepdims=True),
                flux[0:1],
                flux[cells_y - 1 : cells_y],
            )
            for number, row in enumerate(rows):
                send_y[number, line : line + 1] = row


def flat_slots(received, number, capacity):
    senders = received.shape[0]
    part = received[:, number * capacity : (number + 1) * capacity]
    repeats = 128 // capacity
    tiled = jnp.concatenate([part] * repeats, axis=1)
    lane = lax.broadcasted_iota(jnp.int32, (senders, 128), 1) // capacity
    sender = lax.broadcasted_iota(jnp.int32, (senders, 128), 0)
    rows = []
    for group in range(senders // repeats):
        mine = sender == lane + group * repeats
        rows.append(jnp.sum(jnp.where(mine, tiled, 0.0), axis=0, keepdims=True))
    return jnp.concatenate(rows, axis=1)


def middle_kernel(capacity, received, flux_x, flux_y, coef_x_ref, coef_y_ref, out):
    fields, cells_x, cells_y, depth = out.shape
    rows_block = cells_x * cells_y
    shape = (cells_y, depth)
    senders = received.shape[0]
    got = jnp.concatenate([received[sender] for sender in range(senders)], axis=0)
    slots = senders * capacity
    flat = [flat_slots(got, f, capacity) for f in range(fields + 1)]
    cell = flat[fields].astype(jnp.int32)
    row_hot = lax.broadcasted_iota(jnp.int32, (rows_block, slots), 0) == cell // depth
    depth_hot = jnp.where(
        lax.broadcasted_iota(jnp.int32, (depth, slots), 0) == cell % depth, 1.0, 0.0
    ).astype(BF16)
    coef_x = coef_x_ref[...]
    coef_y = coef_y_ref[...]

    def at_x(row, i):
        return jnp.broadcast_to(coef_x[row : row + 1, i : i + 1], shape)

    wide = [jnp.broadcast_to(coef_y[:, row : row + 1], shape) for row in range(7)]
    station = lax.broadcasted_iota(jnp.int32, shape, 0)

    for f in range(fields):
        spread = jnp.where(row_hot, flat[f], 0.0)
        top = spread.astype(BF16)
        rest = (spread - top.astype(F32)).astype(BF16)
        both = lax.dot_general(
            jnp.concatenate([top, rest], axis=0), depth_hot, NT, preferred_element_type=F32
        )
        forcing = both[:rows_block] + both[rows_block:]

        stations = [flux_x[f, i] for i in range(cells_x)]
        before = [None] * cells_x
        after = [None] * cells_x
        for i in range(1, cells_x):
            term = at_x(2, i - 1) * stations[i - 1]
            before[i] = term if i == 1 else before[i - 1] + term
        for i in range(cells_x - 2, -1, -1):
            term = at_x(3, i + 1) * stations[i + 1]
            after[i] = term if i == cells_x - 2 else after[i + 1] + term
        for i in range(cells_x):
            total = at_x(4, i) * stations[i]
            if i > 0:
                total = total + at_x(0, i) * before[i] + at_x(5, i) * stations[i - 1]
            if i < cells_x - 1:
                total = total + at_x(1, i) * after[i] + at_x(6, i) * stations[i + 1]

            line = flux_y[f, i]
            below = wide[2] * line
            above = wide[3] * line
            low = jnp.where(station >= 1, pltpu.roll(line, 1, 0), 0.0)
            high = jnp.where(station < cells_y - 1, pltpu.roll(line, cells_y - 1, 0), 0.0)
            below = jnp.where(station >= 1, pltpu.roll(below, 1, 0), 0.0)
            above = jnp.where(station < cells_y - 1, pltpu.roll(above, cells_y - 1, 0), 0.0)
            step = 1
            while step < cells_y:
                below = below + jnp.where(station >= step, pltpu.roll(below, step, 0), 0.0)
                above = above + jnp.where(
                    station < cells_y - step, pltpu.roll(above, cells_y - step, 0), 0.0
                )
                step *= 2
            total = total + wide[0] * below + wide[1] * above
            total = total + wide[4] * line + wide[5] * low + wide[6] * high
            out[f, i] = forcing[i * cells_y : (i + 1) * cells_y] - total


def last_kernel(turns, base, ends_y, coef_x_ref, coef_y_ref, *refs):
    arrived, out = refs[:-1], refs[-1]
    fields, cells_x, cells_y, depth = out.shape
    shape = (cells_y, depth)
    coef_x = coef_x_ref[...]
    coef_y = coef_y_ref[...]
    place = lax.axis_index("gx")

    def at_x(row, i):
        return jnp.broadcast_to(coef_x[row : row + 1, i : i + 1], shape)

    p_y = jnp.broadcast_to(coef_y[:, 0:1], shape)
    u_y = jnp.broadcast_to(coef_y[:, 1:2], shape)
    station = lax.broadcasted_iota(jnp.int32, shape, 0)
    low_y = jnp.where(station == 0, jnp.broadcast_to(coef_y[:, 5:6], shape), 0.0)
    high_y = jnp.where(station == cells_y - 1, jnp.broadcast_to(coef_y[:, 6:7], shape), 0.0)
    sides = [(place // (1 << (turn.bit_length() - 1))) % 2 == 1 for turn in turns]
    for i in range(cells_x):
        p_x, u_x = at_x(0, i), at_x(1, i)
        low_x, high_x = at_x(5, i), at_x(6, i)
        weights = [jnp.where(upper, p_x, u_x) for upper in sides]
        for f in range(fields):
            total = base[f, i]
            for turn, upper, weight, got in zip(turns, sides, weights, arrived):
                total = total - weight * got[0, f]
                size = 1 << (turn.bit_length() - 1)
                if turn != 2 * size - 1:
                    continue
                if i == 0:
                    near = upper & (place % size == 0)
                    total = total - jnp.where(near, low_x, 0.0) * got[1, f]
                if i == cells_x - 1:
                    near = jnp.logical_not(upper) & (place % size == size - 1)
                    total = total - jnp.where(near, high_x, 0.0) * got[1, f]
            line = f * cells_x + i
            entering = ends_y[0, line : line + 1]
            leaving = ends_y[1, line : line + 1]
            left = ends_y[2, line : line + 1]
            right = ends_y[3, line : line + 1]
            total = total - (p_y * entering + u_y * leaving + low_y * left + high_y * right)
            out[f, i] = total


def swept_y(own):
    count = lax.axis_size("gy")
    place = lax.axis_index("gy")
    zero = jnp.zeros_like(own[0])
    below, above, left, right = zero, zero, zero, zero
    sum_t, sum_u, first, last = own[0], own[1], own[2], own[3]
    bits = count.bit_length() - 1
    for bit in range(bits):
        size = 1 << bit
        pairs = [(i, i ^ (size | 1)) for i in range(count)]
        upper = (place // size) % 2 == 1
        inner = place % size
        if bit == bits - 1 and bit > 0:
            sent = jnp.stack([jnp.where(upper, sum_u, sum_t), jnp.where(upper, first, last)])
            got = lax.ppermute(sent, "gy", pairs)
            got_t = got_u = got[0]
            got_first = got_last = got[1]
        else:
            sent = own if bit == 0 else jnp.stack([sum_t, sum_u, first, last])
            got = lax.ppermute(sent, "gy", pairs)
            got_t, got_u, got_first, got_last = got[0], got[1], got[2], got[3]
        below = jnp.where(upper, below + got_t, below)
        above = jnp.where(upper, above, above + got_u)
        left = jnp.where(upper & (inner == 0), got_last, left)
        right = jnp.where(jnp.logical_not(upper) & (inner == size - 1), got_first, right)
        if bit < bits - 1:
            sum_t, sum_u = sum_t + got_t, sum_u + got_u
            first, last = jnp.where(upper, got_first, first), jnp.where(upper, last, got_last)
    return jnp.stack([below, above, left, right])


def on_device(
    adjoint, jac_x, jac_y, alpha_x, metric_x, alpha_y, metric_y, surf_values, surf_cells, surf_owner
):
    fields, cells_x, cells_y, depth = adjoint.shape
    points = surf_values.shape[2]
    n_x = lax.axis_size("gx")
    devices = n_x * lax.axis_size("gy")
    capacity = max(4, 2 * points // devices)
    sizes = (alpha_x.shape[0], alpha_y.shape[0])
    lanes = -(-max(sizes) // 128) * 128
    width = -(-(fields + 1) * capacity // 128) * 128
    vmem = pl.BlockSpec(memory_space=pltpu.VMEM)
    hbm = pl.BlockSpec(memory_space=pltpu.HBM)

    def array(*shape):
        return jax.ShapeDtypeStruct(shape, F32)

    def kept(arrays):
        return [pltpu.with_memory_space_constraint(a, pltpu.HBM) for a in arrays]

    params = pltpu.CompilerParams(vmem_limit_bytes=24 << 20)
    small = [
        alpha_x.reshape(1, -1),
        alpha_y.reshape(1, -1),
        metric_x.reshape(1, -1),
        metric_y.reshape(1, -1),
        jnp.transpose(surf_values, (1, 0, 2)),
        surf_cells,
        surf_owner.reshape(1, points),
    ]
    pack, coef_x, coef_y = pl.pallas_call(
        functools.partial(points_kernel, sizes, devices, capacity),
        in_specs=[hbm] * len(small),
        out_specs=[vmem] * 3,
        out_shape=[array(devices, 1, width), array(8, 128), array(cells_y, 128)],
        scratch_shapes=[pltpu.VMEM(a.shape, a.dtype) for a in small]
        + [pltpu.VMEM((8, lanes), F32), pltpu.SemaphoreType.DMA((len(small),))],
        compiler_params=params,
        name="points_and_coefficients",
    )(*kept(small))
    received = lax.all_to_all(pack, ("gx", "gy"), 0, 0, tiled=True)

    large = [adjoint, jac_x, jac_y]
    bits = n_x.bit_length() - 1
    flux_x, flux_y, own_y, *faces = pl.pallas_call(
        flux_kernel,
        in_specs=[vmem] * 2 + [hbm] * len(large),
        out_specs=[vmem] * (3 + bits),
        out_shape=[
            array(*adjoint.shape),
            array(*adjoint.shape),
            array(4, fields * cells_x, depth),
        ]
        + [array(2, fields, cells_y, depth)] * bits,
        scratch_shapes=[pltpu.VMEM(a.shape, a.dtype) for a in large]
        + [pltpu.SemaphoreType.DMA((len(large),))],
        compiler_params=params,
        name="flux_and_sums",
    )(coef_x, coef_y, *kept(large))
    turns = tuple(range(n_x - 1, 0, -1))
    arrived = []
    for turn in turns:
        bit = turn.bit_length() - 1
        face = faces[bit] if turn == (2 << bit) - 1 else faces[bit][:1]
        arrived.append(lax.ppermute(face, "gx", [(i, i ^ turn) for i in range(n_x)]))
    ends_y = swept_y(own_y)
    base = pl.pallas_call(
        functools.partial(middle_kernel, capacity),
        in_specs=[vmem] * 5,
        out_specs=vmem,
        out_shape=array(*adjoint.shape),
        compiler_params=params,
        name="forcing_and_block_part",
    )(received, flux_x, flux_y, coef_x, coef_y)
    return pl.pallas_call(
        functools.partial(last_kernel, turns),
        in_specs=[vmem] * (4 + len(turns)),
        out_specs=vmem,
        out_shape=array(*adjoint.shape),
        compiler_params=params,
        name="far_part",
    )(base, ends_y, coef_x, coef_y, *arrived)


def solution(mesh):
    in_specs = (
        P(None, "gx", "gy", None),
        P(None, None, "gx", "gy", None),
        P(None, None, "gx", "gy", None),
        P(),
        P("gx"),
        P(),
        P("gy"),
        P(("gx", "gy"), None, None),
        P(("gx", "gy"), None),
        P(("gx", "gy"), None, None),
    )
    out_specs = P(None, "gx", "gy", None)
    return jax.shard_map(
        on_device, mesh=mesh, in_specs=in_specs, out_specs=out_specs, check_vma=False
    )
```

```python
import functools

import jax
import jax.numpy as jnp
from jax import lax
from jax.experimental import pallas as pl
from jax.experimental.pallas import tpu as pltpu
from jax.sharding import PartitionSpec as P

F32 = jnp.float32
BF16 = jnp.bfloat16
NT = (((1,), (1,)), ((), ()))


def moved(row, by, lane, fill):
    lanes = row.shape[1]
    turned = pltpu.roll(row, by % lanes, 1)
    keep = (lane >= by) if by > 0 else (lane < lanes + by)
    return jnp.where(keep, turned, fill)


def running(parts, lane, direction):
    lanes = lane.shape[1]
    a, b, c, d = parts
    step = 1
    while step < lanes:
        shift = step * direction
        a0, b0 = moved(a, shift, lane, 1.0), moved(b, shift, lane, 0.0)
        c0, d0 = moved(c, shift, lane, 0.0), moved(d, shift, lane, 1.0)
        a, b, c, d = a * a0 + b * c0, a * b0 + b * d0, c * a0 + d * c0, c * b0 + d * d0
        step *= 2
    return a + b


def line_rows(alpha, sizes):
    axes, lanes = alpha.shape
    lane = lax.broadcasted_iota(jnp.int32, (axes, lanes), 1)
    which = lax.broadcasted_iota(jnp.int32, (axes, lanes), 0)
    count = jnp.zeros((axes, lanes), jnp.int32)
    for axis, size in enumerate(sizes):
        count = jnp.where(which == axis, size, count)
    inside = lane < count
    alpha = jnp.where(inside, alpha, 0.5)
    slack = 1.0 - 2.0 * alpha
    twice = 2.0 * alpha

    eps = slack + twice * moved(slack, 1, lane, 0.0)
    c = 1.0 - eps
    fwd = running((1.0 + eps, c, eps, c), lane, 1)
    eps = slack + twice * moved(slack, -1, lane, 0.0)
    c = 1.0 - eps
    bwd = running(
        (
            jnp.where(inside, 1.0 + eps, 1.0),
            jnp.where(inside, c, 0.0),
            jnp.where(inside, eps, 0.0),
            jnp.where(inside, c, 1.0),
        ),
        lane,
        -1,
    )
    weight = twice
    step = 1
    while step < lanes:
        weight = weight * moved(weight, step, lane, 1.0)
        step *= 2
    before_w = moved(weight, 1, lane, 1.0)
    before_f = moved(fwd, 1, lane, 1.0)
    after_g = moved(bwd, -1, lane, 1.0)
    whole = jnp.sum(jnp.where(lane == count - 1, fwd, 0.0), axis=1, keepdims=True)
    sign = jnp.where(lane % 2 == 0, 1.0, -1.0)

    p = jnp.where(inside, sign * weight * after_g, 0.0)
    u = jnp.where(inside, sign * before_f / before_w, 0.0)
    q = jnp.where(inside, 2.0 * sign * before_f / (weight * whole), 0.0)
    v = jnp.where(inside, 2.0 * sign * before_w * after_g / whole, 0.0)
    near = (alpha + 2.0) / 3.0
    far = (4.0 * alpha - 1.0) / 12.0

    def folded(row):
        one, two = row * near, row * far
        return (
            moved(one, 1, lane, 0.0)
            - moved(one, -1, lane, 0.0)
            + moved(two, 2, lane, 0.0)
            - moved(two, -2, lane, 0.0)
        )

    diag = p * (moved(q * near, 1, lane, 0.0) + moved(q * far, 2, lane, 0.0)) - u * (
        moved(v * near, -1, lane, 0.0) + moved(v * far, -2, lane, 0.0)
    )
    next_far = moved(jnp.where(inside, far, 0.0), -1, lane, 0.0)
    last_far = moved(far, 1, lane, 0.0)
    low = (p * moved(q, -1, lane, 0.0) - u * moved(v, -1, lane, 0.0)) * next_far
    high = (p * moved(q, 1, lane, 0.0) - u * moved(v, 1, lane, 0.0)) * last_far
    t = jnp.where(inside, folded(q), 0.0)
    s = jnp.where(inside, folded(v), 0.0)
    return [p, u, t, s, diag, low, high]


def packed_points(values, cells, owners, devices, capacity, width):
    points = owners.shape[1]
    row = lax.broadcasted_iota(jnp.int32, (devices, points), 0)
    hot = jnp.where(row == owners, 1.0, 0.0)
    group = 128
    upper = jnp.where(
        lax.broadcasted_iota(jnp.int32, (group, group), 0)
        < lax.broadcasted_iota(jnp.int32, (group, group), 1),
        1.0,
        0.0,
    ).astype(BF16)
    carried = jnp.zeros((devices, 1), F32)
    ranks = []
    for start in range(0, points, group):
        piece = hot[:, start : start + group]
        counts = carried + jnp.dot(piece.astype(BF16), upper, preferred_element_type=F32)
        ranks.append(jnp.sum(piece * counts, axis=0, keepdims=True))
        carried = carried + jnp.sum(piece, axis=1, keepdims=True)
    rank = jnp.concatenate(ranks, axis=1).astype(jnp.int32)
    slot = lax.broadcasted_iota(jnp.int32, (capacity, points), 0) == rank
    rows = [jnp.where(slot, row, 0.0) for row in values]
    rows.append(jnp.where(slot, cells.astype(F32), 0.0))
    spread = jnp.concatenate(rows, axis=0)
    top = spread.astype(BF16)
    rest = (spread - top.astype(F32)).astype(BF16)
    hot = hot.astype(BF16)
    spare = width - spread.shape[0]
    if spare:
        top = jnp.concatenate([top, jnp.zeros((spare, points), BF16)], axis=0)
        rest = jnp.concatenate([rest, jnp.zeros((spare, points), BF16)], axis=0)
    return lax.dot_general(hot, top, NT, preferred_element_type=F32) + lax.dot_general(
        hot, rest, NT, preferred_element_type=F32
    )


def fetch(sources, targets, sems):
    copies = [
        pltpu.make_async_copy(source, target, sems.at[number])
        for number, (source, target) in enumerate(zip(sources, targets))
    ]
    for copy in copies:
        copy.start()
    return copies


def first_kernel(sizes, capacity, turns, *refs):
    sources, refs = refs[:10], refs[10:]
    flux_x_out, flux_y_out, send_y, coef_x_out, coef_y_out, pack_out = refs[:6]
    faces, targets, alpha_s, pack, sems = refs[6:-13], refs[-13:-3], refs[-3], refs[-2], refs[-1]
    alpha_x, alpha_y, metric_x, metric_y, values, cells, owners, adj, jx, jy = targets
    copies = fetch(sources, targets, sems)
    for copy in copies[:7]:
        copy.wait()
    fields, cells_x, cells_y, depth = adj.shape
    lanes = alpha_s.shape[1]
    place_x = lax.axis_index("gx")
    shape = (cells_y, depth)

    alpha_s[...] = jnp.full(alpha_s.shape, 0.5, F32)
    alpha_s[0:1, 0 : sizes[0]] = alpha_x[...]
    alpha_s[1:2, 0 : sizes[1]] = alpha_y[...]
    rows = line_rows(alpha_s[...], sizes)
    first_x = place_x * cells_x
    first_y = lax.axis_index("gy") * cells_y
    coef_x = jnp.concatenate([row[0:1] for row in rows] + [jnp.zeros((1, lanes), F32)], axis=0)
    coef_y = jnp.concatenate([row[1:2] for row in rows] + [jnp.zeros((1, lanes), F32)], axis=0)
    coef_x = pltpu.roll(coef_x, lax.rem(lanes - first_x, lanes), 1)[:, :128]
    coef_y = pltpu.roll(coef_y, lax.rem(lanes - first_y, lanes), 1)[:, :128]
    row_of = lax.broadcasted_iota(jnp.int32, (8, 128), 0)
    scaled = (row_of != 2) & (row_of != 3)
    gain_x = jnp.concatenate([metric_x[...], jnp.zeros((1, 128 - cells_x), F32)], axis=1)
    gain_y = jnp.concatenate([metric_y[...], jnp.zeros((1, 128 - cells_y), F32)], axis=1)
    coef_x = coef_x * jnp.where(scaled, gain_x, 1.0)
    coef_y = coef_y * jnp.where(scaled, gain_y, 1.0)
    coef_x_out[...] = coef_x
    columns_y = jnp.concatenate([coef_y, jnp.zeros((120, 128), F32)], axis=0).T[:cells_y]
    coef_y_out[...] = columns_y

    devices, _, width = pack.shape
    packed = packed_points(
        [values[f] for f in range(fields)], cells[...], owners[...], devices, capacity, width
    )
    for device in range(devices):
        pack[device] = packed[device : device + 1]
    leaving = pltpu.make_async_copy(pack, pack_out, sems.at[len(sources)])
    leaving.start()

    copies[7].wait()
    copies[8].wait()
    totals = [[None, None] for _ in range(fields)]
    for i in range(cells_x):
        state = [adj[k, i] for k in range(fields)]
        for target in range(fields):
            flux = jx[0, target, i].astype(F32) * state[0]
            for k in range(1, fields):
                flux = flux + jx[k, target, i].astype(F32) * state[k]
            flux_x_out[target, i] = flux
            for side in range(2):
                term = jnp.broadcast_to(coef_x[2 + side : 3 + side, i : i + 1], shape) * flux
                if i > 0:
                    term = totals[target][side] + term
                totals[target][side] = term
    for turn, face in zip(turns, faces):
        size = 1 << (turn.bit_length() - 1)
        upper = (place_x // size) % 2 == 1
        for target in range(fields):
            spot = target * cells_y
            face[spot : spot + cells_y] = jnp.where(upper, totals[target][1], totals[target][0])
            if touches(turn):
                spot = spot + fields * cells_y
                face[spot : spot + cells_y] = jnp.where(
                    upper, flux_x_out[target, 0], flux_x_out[target, cells_x - 1]
                )

    weight_t = jnp.broadcast_to(columns_y[:, 2:3], shape)
    weight_s = jnp.broadcast_to(columns_y[:, 3:4], shape)
    copies[9].wait()
    for i in range(cells_x):
        state = [adj[k, i] for k in range(fields)]
        for target in range(fields):
            flux = jy[0, target, i].astype(F32) * state[0]
            for k in range(1, fields):
                flux = flux + jy[k, target, i].astype(F32) * state[k]
            flux_y_out[target, i] = flux
            line = target * cells_x + i
            rows = (
                jnp.sum(weight_t * flux, axis=0, keepdims=True),
                jnp.sum(weight_s * flux, axis=0, keepdims=True),
                flux[0:1],
                flux[cells_y - 1 : cells_y],
            )
            for number, row in enumerate(rows):
                send_y[number, line : line + 1] = row
    leaving.wait()


def flat_slots(received, number, capacity):
    senders = received.shape[0]
    part = received[:, number * capacity : (number + 1) * capacity]
    repeats = 128 // capacity
    tiled = jnp.concatenate([part] * repeats, axis=1)
    lane = lax.broadcasted_iota(jnp.int32, (senders, 128), 1) // capacity
    sender = lax.broadcasted_iota(jnp.int32, (senders, 128), 0)
    rows = []
    for group in range(senders // repeats):
        mine = sender == lane + group * repeats
        rows.append(jnp.sum(jnp.where(mine, tiled, 0.0), axis=0, keepdims=True))
    return jnp.concatenate(rows, axis=1)


def touches(turn):
    return turn & (turn + 1) == 0


def upper_of(place, turn):
    return (place // (1 << (turn.bit_length() - 1))) % 2 == 1


def block_kernel(flux_x, flux_y, coef_x_ref, coef_y_ref, out):
    fields, cells_x, cells_y, depth = out.shape
    shape = (cells_y, depth)
    coef_x = coef_x_ref[...]
    coef_y = coef_y_ref[...]

    def at_x(row, i):
        return jnp.broadcast_to(coef_x[row : row + 1, i : i + 1], shape)

    wide = [jnp.broadcast_to(coef_y[:, row : row + 1], shape) for row in range(7)]
    station = lax.broadcasted_iota(jnp.int32, shape, 0)

    for f in range(fields):
        stations = [flux_x[f, i] for i in range(cells_x)]
        before = [None] * cells_x
        after = [None] * cells_x
        for i in range(1, cells_x):
            term = at_x(2, i - 1) * stations[i - 1]
            before[i] = term if i == 1 else before[i - 1] + term
        for i in range(cells_x - 2, -1, -1):
            term = at_x(3, i + 1) * stations[i + 1]
            after[i] = term if i == cells_x - 2 else after[i + 1] + term
        for i in range(cells_x):
            total = at_x(4, i) * stations[i]
            if i > 0:
                total = total + at_x(0, i) * before[i] + at_x(5, i) * stations[i - 1]
            if i < cells_x - 1:
                total = total + at_x(1, i) * after[i] + at_x(6, i) * stations[i + 1]

            line = flux_y[f, i]
            below = wide[2] * line
            above = wide[3] * line
            low = jnp.where(station >= 1, pltpu.roll(line, 1, 0), 0.0)
            high = jnp.where(station < cells_y - 1, pltpu.roll(line, cells_y - 1, 0), 0.0)
            below = jnp.where(station >= 1, pltpu.roll(below, 1, 0), 0.0)
            above = jnp.where(station < cells_y - 1, pltpu.roll(above, cells_y - 1, 0), 0.0)
            step = 1
            while step < cells_y:
                below = below + jnp.where(station >= step, pltpu.roll(below, step, 0), 0.0)
                above = above + jnp.where(
                    station < cells_y - step, pltpu.roll(above, cells_y - step, 0), 0.0
                )
                step *= 2
            total = total + wide[0] * below + wide[1] * above
            total = total + wide[4] * line + wide[5] * low + wide[6] * high
            out[f, i] = total


def far_x_kernel(turns_x, base, coef_x_ref, *refs):
    arrived_x, out = refs[:-1], refs[-1]
    fields, cells_x, cells_y, depth = out.shape
    shape = (cells_y, depth)
    coef_x = coef_x_ref[...]
    place = lax.axis_index("gx")
    sides = [upper_of(place, turn) for turn in turns_x]

    def at_x(row, i):
        return jnp.broadcast_to(coef_x[row : row + 1, i : i + 1], shape)

    for f in range(fields):
        for i in range(cells_x):
            total = base[f, i]
            for turn, upper, face in zip(turns_x, sides, arrived_x):
                spot = f * cells_y
                weight = jnp.where(upper, at_x(0, i), at_x(1, i))
                total = total + weight * face[spot : spot + cells_y]
                if not touches(turn):
                    continue
                size = (turn + 1) // 2
                spot = spot + fields * cells_y
                if i == 0:
                    near = upper & (place % size == 0)
                    total = total + jnp.where(near, at_x(5, i), 0.0) * face[spot : spot + cells_y]
                if i == cells_x - 1:
                    near = jnp.logical_not(upper) & (place % size == size - 1)
                    total = total + jnp.where(near, at_x(6, i), 0.0) * face[spot : spot + cells_y]
            out[f, i] = total


def place_kernel(capacity, received, out):
    fields, cells_x, cells_y, depth = out.shape
    rows_block = cells_x * cells_y
    got = jnp.concatenate([received[sender] for sender in range(received.shape[0])], axis=0)
    slots = got.shape[0] * capacity
    flat = [flat_slots(got, f, capacity) for f in range(fields + 1)]
    cell = flat[fields].astype(jnp.int32)
    row_hot = lax.broadcasted_iota(jnp.int32, (rows_block, slots), 0) == cell // depth
    depth_hot = jnp.where(
        lax.broadcasted_iota(jnp.int32, (depth, slots), 0) == cell % depth, 1.0, 0.0
    ).astype(BF16)
    halves = []
    for f in range(fields):
        spread = jnp.where(row_hot, flat[f], 0.0)
        top = spread.astype(BF16)
        halves += [top, (spread - top.astype(F32)).astype(BF16)]
    both = lax.dot_general(
        jnp.concatenate(halves, axis=0), depth_hot, NT, preferred_element_type=F32
    )
    for f in range(fields):
        top = both[2 * f * rows_block : (2 * f + 1) * rows_block]
        forcing = top + both[(2 * f + 1) * rows_block : (2 * f + 2) * rows_block]
        for i in range(cells_x):
            out[f, i] = forcing[i * cells_y : (i + 1) * cells_y]


def last_kernel(turns_z, forcing, base, pair, coef_y_ref, *refs):
    arrived_z, out = refs[:-3], refs[-3]
    held, sems = refs[-2:]
    fields, cells_x, cells_y, depth = out.shape
    shape = (cells_y, depth)
    chip = lax.axis_index("gy") // 2
    odd = lax.axis_index("gy") % 2 == 1

    entering = jnp.where(odd, pair[0], 0.0)
    leaving = jnp.where(odd, 0.0, pair[1])
    left = jnp.where(odd, pair[3], 0.0)
    right = jnp.where(odd, 0.0, pair[2])
    for turn, got in zip(turns_z, arrived_z):
        upper = upper_of(chip, turn)
        entering = entering + jnp.where(upper, got[0], 0.0)
        leaving = leaving + jnp.where(upper, 0.0, got[0])
        if touches(turn):
            size = (turn + 1) // 2
            first = jnp.logical_not(odd) & upper & (chip % size == 0)
            last = odd & jnp.logical_not(upper) & (chip % size == size - 1)
            left = jnp.where(first, got[1], left)
            right = jnp.where(last, got[1], right)

    coef_y = coef_y_ref[...]

    p_y = jnp.broadcast_to(coef_y[:, 0:1], shape)
    u_y = jnp.broadcast_to(coef_y[:, 1:2], shape)
    station = lax.broadcasted_iota(jnp.int32, shape, 0)
    low_y = jnp.where(station == 0, jnp.broadcast_to(coef_y[:, 5:6], shape), 0.0)
    high_y = jnp.where(station == cells_y - 1, jnp.broadcast_to(coef_y[:, 6:7], shape), 0.0)
    copies = []
    for f in range(fields):
        for i in range(cells_x):
            total = base[f, i]
            line = slice(f * cells_x + i, f * cells_x + i + 1)
            total = total + p_y * entering[line] + u_y * leaving[line]
            total = total + low_y * left[line] + high_y * right[line]
            held[f, i] = forcing[f, i] - total
        copies.append(pltpu.make_async_copy(held.at[f], out.at[f], sems.at[f]))
        copies[-1].start()
    for copy in copies:
        copy.wait()


def along_z(own, pair, turns):
    count = lax.axis_size("gy")
    place = lax.axis_index("gy")
    odd = place % 2 == 1
    sum_t, sum_u = own[0] + pair[0], own[1] + pair[1]
    first, last = jnp.where(odd, pair[2], own[2]), jnp.where(odd, own[3], pair[3])
    sent = {}
    for turn in turns:
        bit = turn.bit_length()
        if bit not in sent:
            upper = upper_of(place // 2, turn)
            sent[bit] = jnp.stack([jnp.where(upper, sum_u, sum_t), jnp.where(upper, first, last)])
    return [
        lax.ppermute(sent[turn.bit_length()], "gy", [(i, i ^ (2 * turn + 1)) for i in range(count)])
        for turn in turns
    ]


def on_device(
    adjoint, jac_x, jac_y, alpha_x, metric_x, alpha_y, metric_y, surf_values, surf_cells, surf_owner
):
    fields, cells_x, cells_y, depth = adjoint.shape
    points = surf_values.shape[2]
    n_x = lax.axis_size("gx")
    n_y = lax.axis_size("gy")
    devices = n_x * n_y
    capacity = max(4, 2 * points // devices)
    sizes = (alpha_x.shape[0], alpha_y.shape[0])
    lanes = -(-max(sizes) // 128) * 128
    lines = fields * cells_x
    vmem = pl.BlockSpec(memory_space=pltpu.VMEM)
    hbm = pl.BlockSpec(memory_space=pltpu.HBM)

    def array(*shape):
        return jax.ShapeDtypeStruct(shape, F32)

    def cost(micros):
        return pl.CostEstimate(
            flops=int(micros * 1e9), bytes_accessed=int(micros * 3.6e6), transcendentals=0
        )

    params = pltpu.CompilerParams(vmem_limit_bytes=24 << 20)
    inputs = [
        alpha_x.reshape(1, -1),
        alpha_y.reshape(1, -1),
        metric_x.reshape(1, -1),
        metric_y.reshape(1, -1),
        jnp.transpose(surf_values, (1, 0, 2)),
        surf_cells,
        surf_owner.reshape(1, points),
        adjoint,
        jac_x,
        jac_y,
    ]
    turns_x = tuple(range(n_x - 1, 0, -1))
    turns_z = tuple(range(n_y // 2 - 1, 0, -1))
    width = -(-(fields + 1) * capacity // 128) * 128
    face_rows = fields * cells_y
    flux_x, flux_y, own_y, coef_x, coef_y, pack, *faces = pl.pallas_call(
        functools.partial(first_kernel, sizes, capacity, turns_x),
        in_specs=[hbm] * len(inputs),
        out_specs=[vmem] * 5 + [pl.BlockSpec(memory_space=pl.ANY)] + [vmem] * len(turns_x),
        out_shape=[
            array(*adjoint.shape),
            array(*adjoint.shape),
            array(4, lines, depth),
            array(8, 128),
            array(cells_y, 128),
            array(devices, 1, width),
        ]
        + [array((2 if touches(turn) else 1) * face_rows, depth) for turn in turns_x],
        scratch_shapes=[pltpu.VMEM(a.shape, a.dtype) for a in inputs]
        + [
            pltpu.VMEM((8, lanes), F32),
            pltpu.VMEM((devices, 1, width), F32),
            pltpu.SemaphoreType.DMA((len(inputs) + 1,)),
        ],
        compiler_params=params,
        cost_estimate=cost(2.5),
        name="flux_and_sums",
    )(*[pltpu.with_memory_space_constraint(a, pltpu.HBM) for a in inputs])
    received = lax.all_to_all(pack, ("gx", "gy"), 0, 0, tiled=True)
    arrived_x = [
        lax.ppermute(face, "gx", [(i, i ^ turn) for i in range(n_x)])
        for turn, face in zip(turns_x, faces)
    ]
    pair = lax.ppermute(own_y, "gy", [(i, i ^ 1) for i in range(n_y)])
    arrived_z = along_z(own_y, pair, turns_z)
    base = pl.pallas_call(
        block_kernel,
        in_specs=[vmem] * 4,
        out_specs=vmem,
        out_shape=array(*adjoint.shape),
        compiler_params=params,
        cost_estimate=cost(5),
        name="block_part",
    )(flux_x, flux_y, coef_x, coef_y)
    base = pl.pallas_call(
        functools.partial(far_x_kernel, turns_x),
        in_specs=[vmem] * (2 + len(turns_x)),
        out_specs=vmem,
        out_shape=array(*adjoint.shape),
        compiler_params=params,
        cost_estimate=cost(0.01),
        name="far_x_part",
    )(base, coef_x, *arrived_x)
    forcing = pl.pallas_call(
        functools.partial(place_kernel, capacity),
        in_specs=[vmem],
        out_specs=vmem,
        out_shape=array(*adjoint.shape),
        compiler_params=params,
        cost_estimate=cost(0.01),
        name="placed_points",
    )(received)
    return pl.pallas_call(
        functools.partial(last_kernel, turns_z),
        in_specs=[vmem] * (4 + len(turns_z)),
        out_specs=pl.BlockSpec(memory_space=pl.ANY),
        out_shape=array(*adjoint.shape),
        scratch_shapes=[
            pltpu.VMEM(adjoint.shape, F32),
            pltpu.SemaphoreType.DMA((fields,)),
        ],
        compiler_params=params,
        cost_estimate=cost(1),
        name="far_part",
    )(forcing, base, pair, coef_y, *arrived_z)


def solution(mesh):
    in_specs = (
        P(None, "gx", "gy", None),
        P(None, None, "gx", "gy", None),
        P(None, None, "gx", "gy", None),
        P(),
        P("gx"),
        P(),
        P("gy"),
        P(("gx", "gy"), None, None),
        P(("gx", "gy"), None),
        P(("gx", "gy"), None, None),
    )
    out_specs = P(None, "gx", "gy", None)
    return jax.shard_map(
        on_device, mesh=mesh, in_specs=in_specs, out_specs=out_specs, check_vma=False
    )
```

```python
import functools

import jax
import jax.numpy as jnp
from jax import lax
from jax.experimental import pallas as pl
from jax.experimental.pallas import tpu as pltpu
from jax.sharding import PartitionSpec as P

F32 = jnp.float32
BF16 = jnp.bfloat16
NT = (((1,), (1,)), ((), ()))


def moved(row, by, lane, fill):
    lanes = row.shape[1]
    turned = pltpu.roll(row, by % lanes, 1)
    keep = (lane >= by) if by > 0 else (lane < lanes + by)
    return jnp.where(keep, turned, fill)


def running(parts, lane, direction):
    lanes = lane.shape[1]
    a, b, c, d = parts
    step = 1
    while step < lanes:
        shift = step * direction
        a0, b0 = moved(a, shift, lane, 1.0), moved(b, shift, lane, 0.0)
        c0, d0 = moved(c, shift, lane, 0.0), moved(d, shift, lane, 1.0)
        a, b, c, d = a * a0 + b * c0, a * b0 + b * d0, c * a0 + d * c0, c * b0 + d * d0
        step *= 2
    return a + b


def line_rows(alpha, sizes):
    axes, lanes = alpha.shape
    lane = lax.broadcasted_iota(jnp.int32, (axes, lanes), 1)
    which = lax.broadcasted_iota(jnp.int32, (axes, lanes), 0)
    count = jnp.zeros((axes, lanes), jnp.int32)
    for axis, size in enumerate(sizes):
        count = jnp.where(which == axis, size, count)
    inside = lane < count
    alpha = jnp.where(inside, alpha, 0.5)
    slack = 1.0 - 2.0 * alpha
    twice = 2.0 * alpha

    eps = slack + twice * moved(slack, 1, lane, 0.0)
    c = 1.0 - eps
    fwd = running((1.0 + eps, c, eps, c), lane, 1)
    eps = slack + twice * moved(slack, -1, lane, 0.0)
    c = 1.0 - eps
    bwd = running(
        (
            jnp.where(inside, 1.0 + eps, 1.0),
            jnp.where(inside, c, 0.0),
            jnp.where(inside, eps, 0.0),
            jnp.where(inside, c, 1.0),
        ),
        lane,
        -1,
    )
    weight = twice
    step = 1
    while step < lanes:
        weight = weight * moved(weight, step, lane, 1.0)
        step *= 2
    before_w = moved(weight, 1, lane, 1.0)
    before_f = moved(fwd, 1, lane, 1.0)
    after_g = moved(bwd, -1, lane, 1.0)
    whole = jnp.sum(jnp.where(lane == count - 1, fwd, 0.0), axis=1, keepdims=True)
    sign = jnp.where(lane % 2 == 0, 1.0, -1.0)

    p = jnp.where(inside, sign * weight * after_g, 0.0)
    u = jnp.where(inside, sign * before_f / before_w, 0.0)
    q = jnp.where(inside, 2.0 * sign * before_f / (weight * whole), 0.0)
    v = jnp.where(inside, 2.0 * sign * before_w * after_g / whole, 0.0)
    near = (alpha + 2.0) / 3.0
    far = (4.0 * alpha - 1.0) / 12.0

    def folded(row):
        one, two = row * near, row * far
        return (
            moved(one, 1, lane, 0.0)
            - moved(one, -1, lane, 0.0)
            + moved(two, 2, lane, 0.0)
            - moved(two, -2, lane, 0.0)
        )

    diag = p * (moved(q * near, 1, lane, 0.0) + moved(q * far, 2, lane, 0.0)) - u * (
        moved(v * near, -1, lane, 0.0) + moved(v * far, -2, lane, 0.0)
    )
    next_far = moved(jnp.where(inside, far, 0.0), -1, lane, 0.0)
    last_far = moved(far, 1, lane, 0.0)
    low = (p * moved(q, -1, lane, 0.0) - u * moved(v, -1, lane, 0.0)) * next_far
    high = (p * moved(q, 1, lane, 0.0) - u * moved(v, 1, lane, 0.0)) * last_far
    t = jnp.where(inside, folded(q), 0.0)
    s = jnp.where(inside, folded(v), 0.0)
    return [p, u, t, s, diag, low, high]


def packed_points(values, cells, owners, devices, capacity, width):
    points = owners.shape[1]
    row = lax.broadcasted_iota(jnp.int32, (devices, points), 0)
    hot = jnp.where(row == owners, 1.0, 0.0)
    group = 128
    upper = jnp.where(
        lax.broadcasted_iota(jnp.int32, (group, group), 0)
        < lax.broadcasted_iota(jnp.int32, (group, group), 1),
        1.0,
        0.0,
    ).astype(BF16)
    carried = jnp.zeros((devices, 1), F32)
    ranks = []
    for start in range(0, points, group):
        piece = hot[:, start : start + group]
        counts = carried + jnp.dot(piece.astype(BF16), upper, preferred_element_type=F32)
        ranks.append(jnp.sum(piece * counts, axis=0, keepdims=True))
        carried = carried + jnp.sum(piece, axis=1, keepdims=True)
    rank = jnp.concatenate(ranks, axis=1).astype(jnp.int32)
    slot = lax.broadcasted_iota(jnp.int32, (capacity, points), 0) == rank
    rows = [jnp.where(slot, row, 0.0) for row in values]
    rows.append(jnp.where(slot, cells.astype(F32), 0.0))
    spread = jnp.concatenate(rows, axis=0)
    top = spread.astype(BF16)
    rest = (spread - top.astype(F32)).astype(BF16)
    hot = hot.astype(BF16)
    spare = width - spread.shape[0]
    if spare:
        top = jnp.concatenate([top, jnp.zeros((spare, points), BF16)], axis=0)
        rest = jnp.concatenate([rest, jnp.zeros((spare, points), BF16)], axis=0)
    return lax.dot_general(hot, top, NT, preferred_element_type=F32) + lax.dot_general(
        hot, rest, NT, preferred_element_type=F32
    )


def fetch(sources, targets, sems):
    copies = [
        pltpu.make_async_copy(source, target, sems.at[number])
        for number, (source, target) in enumerate(zip(sources, targets))
    ]
    for copy in copies:
        copy.start()
    return copies


def first_kernel(sizes, capacity, turns, *refs):
    sources, refs = refs[:10], refs[10:]
    flux_x_out, flux_y_out, send_y, coef_x_out, coef_y_out, pack_out = refs[:6]
    faces, targets, alpha_s, pack, sems = refs[6:-13], refs[-13:-3], refs[-3], refs[-2], refs[-1]
    alpha_x, alpha_y, metric_x, metric_y, values, cells, owners, adj, jx, jy = targets
    copies = fetch(sources, targets, sems)
    for copy in copies[:7]:
        copy.wait()
    fields, cells_x, cells_y, depth = adj.shape
    lanes = alpha_s.shape[1]
    place_x = lax.axis_index("gx")
    shape = (cells_y, depth)

    alpha_s[...] = jnp.full(alpha_s.shape, 0.5, F32)
    alpha_s[0:1, 0 : sizes[0]] = alpha_x[...]
    alpha_s[1:2, 0 : sizes[1]] = alpha_y[...]
    rows = line_rows(alpha_s[...], sizes)
    first_x = place_x * cells_x
    first_y = lax.axis_index("gy") * cells_y
    coef_x = jnp.concatenate([row[0:1] for row in rows] + [jnp.zeros((1, lanes), F32)], axis=0)
    coef_y = jnp.concatenate([row[1:2] for row in rows] + [jnp.zeros((1, lanes), F32)], axis=0)
    coef_x = pltpu.roll(coef_x, lax.rem(lanes - first_x, lanes), 1)[:, :128]
    coef_y = pltpu.roll(coef_y, lax.rem(lanes - first_y, lanes), 1)[:, :128]
    row_of = lax.broadcasted_iota(jnp.int32, (8, 128), 0)
    scaled = (row_of != 2) & (row_of != 3)
    gain_x = jnp.concatenate([metric_x[...], jnp.zeros((1, 128 - cells_x), F32)], axis=1)
    gain_y = jnp.concatenate([metric_y[...], jnp.zeros((1, 128 - cells_y), F32)], axis=1)
    coef_x = coef_x * jnp.where(scaled, gain_x, 1.0)
    coef_y = coef_y * jnp.where(scaled, gain_y, 1.0)
    coef_x_out[...] = coef_x
    columns_y = jnp.concatenate([coef_y, jnp.zeros((120, 128), F32)], axis=0).T[:cells_y]
    coef_y_out[...] = columns_y

    devices, _, width = pack.shape
    packed = packed_points(
        [values[f] for f in range(fields)], cells[...], owners[...], devices, capacity, width
    )
    for device in range(devices):
        pack[device] = packed[device : device + 1]
    leaving = pltpu.make_async_copy(pack, pack_out, sems.at[len(sources)])
    leaving.start()

    copies[7].wait()
    copies[8].wait()
    totals = [[None, None] for _ in range(fields)]
    for i in range(cells_x):
        state = [adj[k, i] for k in range(fields)]
        for target in range(fields):
            flux = jx[0, target, i].astype(F32) * state[0]
            for k in range(1, fields):
                flux = flux + jx[k, target, i].astype(F32) * state[k]
            flux_x_out[target, i] = flux
            for side in range(2):
                term = jnp.broadcast_to(coef_x[2 + side : 3 + side, i : i + 1], shape) * flux
                if i > 0:
                    term = totals[target][side] + term
                totals[target][side] = term
    for turn, face in zip(turns, faces):
        size = 1 << (turn.bit_length() - 1)
        upper = (place_x // size) % 2 == 1
        for target in range(fields):
            spot = target * cells_y
            face[spot : spot + cells_y] = jnp.where(upper, totals[target][1], totals[target][0])
            if touches(turn):
                spot = spot + fields * cells_y
                face[spot : spot + cells_y] = jnp.where(
                    upper, flux_x_out[target, 0], flux_x_out[target, cells_x - 1]
                )

    weight_t = jnp.broadcast_to(columns_y[:, 2:3], shape)
    weight_s = jnp.broadcast_to(columns_y[:, 3:4], shape)
    copies[9].wait()
    for i in range(cells_x):
        state = [adj[k, i] for k in range(fields)]
        for target in range(fields):
            flux = jy[0, target, i].astype(F32) * state[0]
            for k in range(1, fields):
                flux = flux + jy[k, target, i].astype(F32) * state[k]
            flux_y_out[target, i] = flux
            line = target * cells_x + i
            rows = (
                jnp.sum(weight_t * flux, axis=0, keepdims=True),
                jnp.sum(weight_s * flux, axis=0, keepdims=True),
                flux[0:1],
                flux[cells_y - 1 : cells_y],
            )
            for number, row in enumerate(rows):
                send_y[number, line : line + 1] = row
    leaving.wait()


def flat_slots(received, number, capacity):
    senders = received.shape[0]
    part = received[:, number * capacity : (number + 1) * capacity]
    repeats = 128 // capacity
    tiled = jnp.concatenate([part] * repeats, axis=1)
    lane = lax.broadcasted_iota(jnp.int32, (senders, 128), 1) // capacity
    sender = lax.broadcasted_iota(jnp.int32, (senders, 128), 0)
    rows = []
    for group in range(senders // repeats):
        mine = sender == lane + group * repeats
        rows.append(jnp.sum(jnp.where(mine, tiled, 0.0), axis=0, keepdims=True))
    return jnp.concatenate(rows, axis=1)


def touches(turn):
    return turn & (turn + 1) == 0


def upper_of(place, turn):
    return (place // (1 << (turn.bit_length() - 1))) % 2 == 1


def block_kernel(flux_x, flux_y, coef_x_ref, coef_y_ref, out):
    fields, cells_x, cells_y, depth = out.shape
    shape = (cells_y, depth)
    coef_x = coef_x_ref[...]
    coef_y = coef_y_ref[...]

    def at_x(row, i):
        return jnp.broadcast_to(coef_x[row : row + 1, i : i + 1], shape)

    wide = [jnp.broadcast_to(coef_y[:, row : row + 1], shape) for row in range(7)]
    station = lax.broadcasted_iota(jnp.int32, shape, 0)

    for f in range(fields):
        stations = [flux_x[f, i] for i in range(cells_x)]
        before = [None] * cells_x
        after = [None] * cells_x
        for i in range(1, cells_x):
            term = at_x(2, i - 1) * stations[i - 1]
            before[i] = term if i == 1 else before[i - 1] + term
        for i in range(cells_x - 2, -1, -1):
            term = at_x(3, i + 1) * stations[i + 1]
            after[i] = term if i == cells_x - 2 else after[i + 1] + term
        for i in range(cells_x):
            total = at_x(4, i) * stations[i]
            if i > 0:
                total = total + at_x(0, i) * before[i] + at_x(5, i) * stations[i - 1]
            if i < cells_x - 1:
                total = total + at_x(1, i) * after[i] + at_x(6, i) * stations[i + 1]

            line = flux_y[f, i]
            below = wide[2] * line
            above = wide[3] * line
            low = jnp.where(station >= 1, pltpu.roll(line, 1, 0), 0.0)
            high = jnp.where(station < cells_y - 1, pltpu.roll(line, cells_y - 1, 0), 0.0)
            below = jnp.where(station >= 1, pltpu.roll(below, 1, 0), 0.0)
            above = jnp.where(station < cells_y - 1, pltpu.roll(above, cells_y - 1, 0), 0.0)
            step = 1
            while step < cells_y:
                below = below + jnp.where(station >= step, pltpu.roll(below, step, 0), 0.0)
                above = above + jnp.where(
                    station < cells_y - step, pltpu.roll(above, cells_y - step, 0), 0.0
                )
                step *= 2
            total = total + wide[0] * below + wide[1] * above
            total = total + wide[4] * line + wide[5] * low + wide[6] * high
            out[f, i] = total


def far_x_kernel(turns_x, base, coef_x_ref, *refs):
    arrived_x, out = refs[:-1], refs[-1]
    fields, cells_x, cells_y, depth = out.shape
    shape = (cells_y, depth)
    coef_x = coef_x_ref[...]
    place = lax.axis_index("gx")
    sides = [upper_of(place, turn) for turn in turns_x]

    def at_x(row, i):
        return jnp.broadcast_to(coef_x[row : row + 1, i : i + 1], shape)

    for f in range(fields):
        for i in range(cells_x):
            total = base[f, i]
            for turn, upper, face in zip(turns_x, sides, arrived_x):
                spot = f * cells_y
                weight = jnp.where(upper, at_x(0, i), at_x(1, i))
                total = total + weight * face[spot : spot + cells_y]
                if not touches(turn):
                    continue
                size = (turn + 1) // 2
                spot = spot + fields * cells_y
                if i == 0:
                    near = upper & (place % size == 0)
                    total = total + jnp.where(near, at_x(5, i), 0.0) * face[spot : spot + cells_y]
                if i == cells_x - 1:
                    near = jnp.logical_not(upper) & (place % size == size - 1)
                    total = total + jnp.where(near, at_x(6, i), 0.0) * face[spot : spot + cells_y]
            out[f, i] = total


def place_kernel(capacity, received, out):
    fields, cells_x, cells_y, depth = out.shape
    rows_block = cells_x * cells_y
    got = jnp.concatenate([received[sender] for sender in range(received.shape[0])], axis=0)
    slots = got.shape[0] * capacity
    flat = [flat_slots(got, f, capacity) for f in range(fields + 1)]
    cell = flat[fields].astype(jnp.int32)
    row_hot = lax.broadcasted_iota(jnp.int32, (rows_block, slots), 0) == cell // depth
    depth_hot = jnp.where(
        lax.broadcasted_iota(jnp.int32, (depth, slots), 0) == cell % depth, 1.0, 0.0
    ).astype(BF16)
    halves = []
    for f in range(fields):
        spread = jnp.where(row_hot, flat[f], 0.0)
        top = spread.astype(BF16)
        halves += [top, (spread - top.astype(F32)).astype(BF16)]
    both = lax.dot_general(
        jnp.concatenate(halves, axis=0), depth_hot, NT, preferred_element_type=F32
    )
    for f in range(fields):
        top = both[2 * f * rows_block : (2 * f + 1) * rows_block]
        forcing = top + both[(2 * f + 1) * rows_block : (2 * f + 2) * rows_block]
        for i in range(cells_x):
            out[f, i] = forcing[i * cells_y : (i + 1) * cells_y]


def last_kernel(turns_z, forcing, base, pair, coef_y_ref, *refs):
    arrived_z, out = refs[:-3], refs[-3]
    held, sems = refs[-2:]
    fields, cells_x, cells_y, depth = out.shape
    shape = (cells_y, depth)
    chip = lax.axis_index("gy") // 2
    odd = lax.axis_index("gy") % 2 == 1

    entering = jnp.where(odd, pair[0], 0.0)
    leaving = jnp.where(odd, 0.0, pair[1])
    left = jnp.where(odd, pair[3], 0.0)
    right = jnp.where(odd, 0.0, pair[2])
    for turn, got in zip(turns_z, arrived_z):
        upper = upper_of(chip, turn)
        entering = entering + jnp.where(upper, got[0], 0.0)
        leaving = leaving + jnp.where(upper, 0.0, got[0])
        if touches(turn):
            size = (turn + 1) // 2
            first = jnp.logical_not(odd) & upper & (chip % size == 0)
            last = odd & jnp.logical_not(upper) & (chip % size == size - 1)
            left = jnp.where(first, got[1], left)
            right = jnp.where(last, got[1], right)

    coef_y = coef_y_ref[...]

    p_y = jnp.broadcast_to(coef_y[:, 0:1], shape)
    u_y = jnp.broadcast_to(coef_y[:, 1:2], shape)
    station = lax.broadcasted_iota(jnp.int32, shape, 0)
    low_y = jnp.where(station == 0, jnp.broadcast_to(coef_y[:, 5:6], shape), 0.0)
    high_y = jnp.where(station == cells_y - 1, jnp.broadcast_to(coef_y[:, 6:7], shape), 0.0)
    copies = []
    for f in range(fields):
        for i in range(cells_x):
            total = base[f, i]
            line = slice(f * cells_x + i, f * cells_x + i + 1)
            total = total + p_y * entering[line] + u_y * leaving[line]
            total = total + low_y * left[line] + high_y * right[line]
            held[f, i] = forcing[f, i] - total
        copies.append(pltpu.make_async_copy(held.at[f], out.at[f], sems.at[f]))
        copies[-1].start()
    for copy in copies:
        copy.wait()


def along_z(own, pair, turns):
    count = lax.axis_size("gy")
    place = lax.axis_index("gy")
    odd = place % 2 == 1
    sum_t, sum_u = own[0] + pair[0], own[1] + pair[1]
    first, last = jnp.where(odd, pair[2], own[2]), jnp.where(odd, own[3], pair[3])
    sent = {}
    for turn in turns:
        bit = turn.bit_length()
        if bit not in sent:
            upper = upper_of(place // 2, turn)
            sent[bit] = jnp.stack([jnp.where(upper, sum_u, sum_t), jnp.where(upper, first, last)])
    return [
        lax.ppermute(sent[turn.bit_length()], "gy", [(i, i ^ (2 * turn + 1)) for i in range(count)])
        for turn in turns
    ]


def on_device(
    adjoint, jac_x, jac_y, alpha_x, metric_x, alpha_y, metric_y, surf_values, surf_cells, surf_owner
):
    fields, cells_x, cells_y, depth = adjoint.shape
    points = surf_values.shape[2]
    n_x = lax.axis_size("gx")
    n_y = lax.axis_size("gy")
    devices = n_x * n_y
    capacity = max(4, 2 * points // devices)
    sizes = (alpha_x.shape[0], alpha_y.shape[0])
    lanes = -(-max(sizes) // 128) * 128
    lines = fields * cells_x
    vmem = pl.BlockSpec(memory_space=pltpu.VMEM)
    hbm = pl.BlockSpec(memory_space=pltpu.HBM)

    def array(*shape):
        return jax.ShapeDtypeStruct(shape, F32)

    def cost(micros):
        return pl.CostEstimate(
            flops=int(micros * 1e9), bytes_accessed=int(micros * 3.6e6), transcendentals=0
        )

    params = pltpu.CompilerParams(vmem_limit_bytes=24 << 20)
    inputs = [
        alpha_x.reshape(1, -1),
        alpha_y.reshape(1, -1),
        metric_x.reshape(1, -1),
        metric_y.reshape(1, -1),
        jnp.transpose(surf_values, (1, 0, 2)),
        surf_cells,
        surf_owner.reshape(1, points),
        adjoint,
        jac_x,
        jac_y,
    ]
    turns_x = tuple(range(n_x - 1, 0, -1))
    turns_z = tuple(range(n_y // 2 - 1, 0, -1))
    width = -(-(fields + 1) * capacity // 128) * 128
    face_rows = fields * cells_y
    flux_x, flux_y, own_y, coef_x, coef_y, pack, *faces = pl.pallas_call(
        functools.partial(first_kernel, sizes, capacity, turns_x),
        in_specs=[hbm] * len(inputs),
        out_specs=[vmem] * 5 + [pl.BlockSpec(memory_space=pl.ANY)] + [vmem] * len(turns_x),
        out_shape=[
            array(*adjoint.shape),
            array(*adjoint.shape),
            array(4, lines, depth),
            array(8, 128),
            array(cells_y, 128),
            array(devices, 1, width),
        ]
        + [array((2 if touches(turn) else 1) * face_rows, depth) for turn in turns_x],
        scratch_shapes=[pltpu.VMEM(a.shape, a.dtype) for a in inputs]
        + [
            pltpu.VMEM((8, lanes), F32),
            pltpu.VMEM((devices, 1, width), F32),
            pltpu.SemaphoreType.DMA((len(inputs) + 1,)),
        ],
        compiler_params=params,
        cost_estimate=cost(2.5),
        name="flux_and_sums",
    )(*[pltpu.with_memory_space_constraint(a, pltpu.HBM) for a in inputs])
    received = lax.all_to_all(pack, ("gx", "gy"), 0, 0, tiled=True)
    arrived = {}
    for turn, face in sorted(zip(turns_x, faces), key=lambda item: not touches(item[0])):
        if not touches(turn):
            face, arrived[1] = lax.optimization_barrier((face, arrived[1]))
        arrived[turn] = lax.ppermute(face, "gx", [(i, i ^ turn) for i in range(n_x)])
    arrived_x = [arrived[turn] for turn in turns_x]
    pair = lax.ppermute(own_y, "gy", [(i, i ^ 1) for i in range(n_y)])
    arrived_z = along_z(own_y, pair, turns_z)
    base = pl.pallas_call(
        block_kernel,
        in_specs=[vmem] * 4,
        out_specs=vmem,
        out_shape=array(*adjoint.shape),
        compiler_params=params,
        cost_estimate=cost(5),
        name="block_part",
    )(flux_x, flux_y, coef_x, coef_y)
    base = pl.pallas_call(
        functools.partial(far_x_kernel, turns_x),
        in_specs=[vmem] * (2 + len(turns_x)),
        out_specs=vmem,
        out_shape=array(*adjoint.shape),
        compiler_params=params,
        cost_estimate=cost(0.01),
        name="far_x_part",
    )(base, coef_x, *arrived_x)
    forcing = pl.pallas_call(
        functools.partial(place_kernel, capacity),
        in_specs=[vmem],
        out_specs=vmem,
        out_shape=array(*adjoint.shape),
        compiler_params=params,
        cost_estimate=cost(0.01),
        name="placed_points",
    )(received)
    return pl.pallas_call(
        functools.partial(last_kernel, turns_z),
        in_specs=[vmem] * (4 + len(turns_z)),
        out_specs=pl.BlockSpec(memory_space=pl.ANY),
        out_shape=array(*adjoint.shape),
        scratch_shapes=[
            pltpu.VMEM(adjoint.shape, F32),
            pltpu.SemaphoreType.DMA((fields,)),
        ],
        compiler_params=params,
        cost_estimate=cost(1),
        name="far_part",
    )(forcing, base, pair, coef_y, *arrived_z)


def solution(mesh):
    in_specs = (
        P(None, "gx", "gy", None),
        P(None, None, "gx", "gy", None),
        P(None, None, "gx", "gy", None),
        P(),
        P("gx"),
        P(),
        P("gy"),
        P(("gx", "gy"), None, None),
        P(("gx", "gy"), None),
        P(("gx", "gy"), None, None),
    )
    out_specs = P(None, "gx", "gy", None)
    return jax.shard_map(
        on_device, mesh=mesh, in_specs=in_specs, out_specs=out_specs, check_vma=False
    )
```

```python
import functools

import jax
import jax.numpy as jnp
from jax import lax
from jax.experimental import pallas as pl
from jax.experimental.pallas import tpu as pltpu
from jax.sharding import PartitionSpec as P

F32 = jnp.float32
BF16 = jnp.bfloat16
NT = (((1,), (1,)), ((), ()))


def moved(row, by, lane, fill):
    lanes = row.shape[1]
    turned = pltpu.roll(row, by % lanes, 1)
    keep = (lane >= by) if by > 0 else (lane < lanes + by)
    return jnp.where(keep, turned, fill)


def running(parts, lane, direction):
    lanes = lane.shape[1]
    a, b, c, d = parts
    step = 1
    while step < lanes:
        shift = step * direction
        a0, b0 = moved(a, shift, lane, 1.0), moved(b, shift, lane, 0.0)
        c0, d0 = moved(c, shift, lane, 0.0), moved(d, shift, lane, 1.0)
        a, b, c, d = a * a0 + b * c0, a * b0 + b * d0, c * a0 + d * c0, c * b0 + d * d0
        step *= 2
    return a + b


def line_rows(alpha, sizes):
    axes, lanes = alpha.shape
    lane = lax.broadcasted_iota(jnp.int32, (axes, lanes), 1)
    which = lax.broadcasted_iota(jnp.int32, (axes, lanes), 0)
    count = jnp.zeros((axes, lanes), jnp.int32)
    for axis, size in enumerate(sizes):
        count = jnp.where(which == axis, size, count)
    inside = lane < count
    alpha = jnp.where(inside, alpha, 0.5)
    slack = 1.0 - 2.0 * alpha
    twice = 2.0 * alpha

    eps = slack + twice * moved(slack, 1, lane, 0.0)
    c = 1.0 - eps
    fwd = running((1.0 + eps, c, eps, c), lane, 1)
    eps = slack + twice * moved(slack, -1, lane, 0.0)
    c = 1.0 - eps
    bwd = running(
        (
            jnp.where(inside, 1.0 + eps, 1.0),
            jnp.where(inside, c, 0.0),
            jnp.where(inside, eps, 0.0),
            jnp.where(inside, c, 1.0),
        ),
        lane,
        -1,
    )
    weight = twice
    step = 1
    while step < lanes:
        weight = weight * moved(weight, step, lane, 1.0)
        step *= 2
    before_w = moved(weight, 1, lane, 1.0)
    before_f = moved(fwd, 1, lane, 1.0)
    after_g = moved(bwd, -1, lane, 1.0)
    whole = jnp.sum(jnp.where(lane == count - 1, fwd, 0.0), axis=1, keepdims=True)
    sign = jnp.where(lane % 2 == 0, 1.0, -1.0)

    p = jnp.where(inside, sign * weight * after_g, 0.0)
    u = jnp.where(inside, sign * before_f / before_w, 0.0)
    q = jnp.where(inside, 2.0 * sign * before_f / (weight * whole), 0.0)
    v = jnp.where(inside, 2.0 * sign * before_w * after_g / whole, 0.0)
    near = (alpha + 2.0) / 3.0
    far = (4.0 * alpha - 1.0) / 12.0

    def folded(row):
        one, two = row * near, row * far
        return (
            moved(one, 1, lane, 0.0)
            - moved(one, -1, lane, 0.0)
            + moved(two, 2, lane, 0.0)
            - moved(two, -2, lane, 0.0)
        )

    diag = p * (moved(q * near, 1, lane, 0.0) + moved(q * far, 2, lane, 0.0)) - u * (
        moved(v * near, -1, lane, 0.0) + moved(v * far, -2, lane, 0.0)
    )
    next_far = moved(jnp.where(inside, far, 0.0), -1, lane, 0.0)
    last_far = moved(far, 1, lane, 0.0)
    low = (p * moved(q, -1, lane, 0.0) - u * moved(v, -1, lane, 0.0)) * next_far
    high = (p * moved(q, 1, lane, 0.0) - u * moved(v, 1, lane, 0.0)) * last_far
    t = jnp.where(inside, folded(q), 0.0)
    s = jnp.where(inside, folded(v), 0.0)
    return [p, u, t, s, diag, low, high]


def packed_points(values, cells, owners, devices, capacity, width):
    points = owners.shape[1]
    row = lax.broadcasted_iota(jnp.int32, (devices, points), 0)
    hot = jnp.where(row == owners, 1.0, 0.0)
    group = 128
    upper = jnp.where(
        lax.broadcasted_iota(jnp.int32, (group, group), 0)
        < lax.broadcasted_iota(jnp.int32, (group, group), 1),
        1.0,
        0.0,
    ).astype(BF16)
    carried = jnp.zeros((devices, 1), F32)
    ranks = []
    for start in range(0, points, group):
        piece = hot[:, start : start + group]
        counts = carried + jnp.dot(piece.astype(BF16), upper, preferred_element_type=F32)
        ranks.append(jnp.sum(piece * counts, axis=0, keepdims=True))
        carried = carried + jnp.sum(piece, axis=1, keepdims=True)
    rank = jnp.concatenate(ranks, axis=1).astype(jnp.int32)
    slot = lax.broadcasted_iota(jnp.int32, (capacity, points), 0) == rank
    rows = [jnp.where(slot, row, 0.0) for row in values]
    rows.append(jnp.where(slot, cells.astype(F32), 0.0))
    spread = jnp.concatenate(rows, axis=0)
    top = spread.astype(BF16)
    rest = (spread - top.astype(F32)).astype(BF16)
    hot = hot.astype(BF16)
    spare = width - spread.shape[0]
    if spare:
        top = jnp.concatenate([top, jnp.zeros((spare, points), BF16)], axis=0)
        rest = jnp.concatenate([rest, jnp.zeros((spare, points), BF16)], axis=0)
    return lax.dot_general(hot, top, NT, preferred_element_type=F32) + lax.dot_general(
        hot, rest, NT, preferred_element_type=F32
    )


def fetch(sources, targets, sems):
    copies = [
        pltpu.make_async_copy(source, target, sems.at[number])
        for number, (source, target) in enumerate(zip(sources, targets))
    ]
    for copy in copies:
        copy.start()
    return copies


def first_kernel(sizes, capacity, turns, *refs):
    sources, refs = refs[:10], refs[10:]
    flux_x_out, flux_y_out, send_y, coef_x_out, coef_y_out, pack_out = refs[:6]
    faces, targets, alpha_s, pack, sems = refs[6:-13], refs[-13:-3], refs[-3], refs[-2], refs[-1]
    alpha_x, alpha_y, metric_x, metric_y, values, cells, owners, adj, jx, jy = targets
    copies = fetch(sources, targets, sems)
    for copy in copies[:7]:
        copy.wait()
    fields, cells_x, cells_y, depth = adj.shape
    lanes = alpha_s.shape[1]
    place_x = lax.axis_index("gx")
    shape = (cells_y, depth)

    alpha_s[...] = jnp.full(alpha_s.shape, 0.5, F32)
    alpha_s[0:1, 0 : sizes[0]] = alpha_x[...]
    alpha_s[1:2, 0 : sizes[1]] = alpha_y[...]
    rows = line_rows(alpha_s[...], sizes)
    first_x = place_x * cells_x
    first_y = lax.axis_index("gy") * cells_y
    coef_x = jnp.concatenate([row[0:1] for row in rows] + [jnp.zeros((1, lanes), F32)], axis=0)
    coef_y = jnp.concatenate([row[1:2] for row in rows] + [jnp.zeros((1, lanes), F32)], axis=0)
    coef_x = pltpu.roll(coef_x, lax.rem(lanes - first_x, lanes), 1)[:, :128]
    coef_y = pltpu.roll(coef_y, lax.rem(lanes - first_y, lanes), 1)[:, :128]
    row_of = lax.broadcasted_iota(jnp.int32, (8, 128), 0)
    scaled = (row_of != 2) & (row_of != 3)
    gain_x = jnp.concatenate([metric_x[...], jnp.zeros((1, 128 - cells_x), F32)], axis=1)
    gain_y = jnp.concatenate([metric_y[...], jnp.zeros((1, 128 - cells_y), F32)], axis=1)
    coef_x = coef_x * jnp.where(scaled, gain_x, 1.0)
    coef_y = coef_y * jnp.where(scaled, gain_y, 1.0)
    coef_x_out[...] = coef_x
    columns_y = jnp.concatenate([coef_y, jnp.zeros((120, 128), F32)], axis=0).T[:cells_y]
    coef_y_out[...] = columns_y

    devices, _, width = pack.shape
    packed = packed_points(
        [values[f] for f in range(fields)], cells[...], owners[...], devices, capacity, width
    )
    for device in range(devices):
        pack[device] = packed[device : device + 1]
    leaving = pltpu.make_async_copy(pack, pack_out, sems.at[len(sources)])
    leaving.start()

    copies[7].wait()
    copies[8].wait()
    totals = [[None, None] for _ in range(fields)]
    for i in range(cells_x):
        state = [adj[k, i] for k in range(fields)]
        for target in range(fields):
            flux = jx[0, target, i].astype(F32) * state[0]
            for k in range(1, fields):
                flux = flux + jx[k, target, i].astype(F32) * state[k]
            flux_x_out[target, i] = flux
            for side in range(2):
                term = jnp.broadcast_to(coef_x[2 + side : 3 + side, i : i + 1], shape) * flux
                if i > 0:
                    term = totals[target][side] + term
                totals[target][side] = term
    for turn, face in zip(turns, faces):
        size = 1 << (turn.bit_length() - 1)
        upper = (place_x // size) % 2 == 1
        for target in range(fields):
            spot = target * cells_y
            face[spot : spot + cells_y] = jnp.where(upper, totals[target][1], totals[target][0])
            if touches(turn):
                spot = spot + fields * cells_y
                face[spot : spot + cells_y] = jnp.where(
                    upper, flux_x_out[target, 0], flux_x_out[target, cells_x - 1]
                )

    weight_t = jnp.broadcast_to(columns_y[:, 2:3], shape)
    weight_s = jnp.broadcast_to(columns_y[:, 3:4], shape)
    copies[9].wait()
    for i in range(cells_x):
        state = [adj[k, i] for k in range(fields)]
        for target in range(fields):
            flux = jy[0, target, i].astype(F32) * state[0]
            for k in range(1, fields):
                flux = flux + jy[k, target, i].astype(F32) * state[k]
            flux_y_out[target, i] = flux
            line = target * cells_x + i
            rows = (
                jnp.sum(weight_t * flux, axis=0, keepdims=True),
                jnp.sum(weight_s * flux, axis=0, keepdims=True),
                flux[0:1],
                flux[cells_y - 1 : cells_y],
            )
            for number, row in enumerate(rows):
                send_y[number, line : line + 1] = row
    leaving.wait()


def flat_slots(received, number, capacity):
    senders = received.shape[0]
    part = received[:, number * capacity : (number + 1) * capacity]
    repeats = 128 // capacity
    tiled = jnp.concatenate([part] * repeats, axis=1)
    lane = lax.broadcasted_iota(jnp.int32, (senders, 128), 1) // capacity
    sender = lax.broadcasted_iota(jnp.int32, (senders, 128), 0)
    rows = []
    for group in range(senders // repeats):
        mine = sender == lane + group * repeats
        rows.append(jnp.sum(jnp.where(mine, tiled, 0.0), axis=0, keepdims=True))
    return jnp.concatenate(rows, axis=1)


def touches(turn):
    return turn & (turn + 1) == 0


def upper_of(place, turn):
    return (place // (1 << (turn.bit_length() - 1))) % 2 == 1


def block_kernel(flux_x, flux_y, coef_x_ref, coef_y_ref, out):
    fields, cells_x, cells_y, depth = out.shape
    shape = (cells_y, depth)
    coef_x = coef_x_ref[...]
    coef_y = coef_y_ref[...]

    def at_x(row, i):
        return jnp.broadcast_to(coef_x[row : row + 1, i : i + 1], shape)

    wide = [jnp.broadcast_to(coef_y[:, row : row + 1], shape) for row in range(7)]
    station = lax.broadcasted_iota(jnp.int32, shape, 0)

    for f in range(fields):
        stations = [flux_x[f, i] for i in range(cells_x)]
        before = [None] * cells_x
        after = [None] * cells_x
        for i in range(1, cells_x):
            term = at_x(2, i - 1) * stations[i - 1]
            before[i] = term if i == 1 else before[i - 1] + term
        for i in range(cells_x - 2, -1, -1):
            term = at_x(3, i + 1) * stations[i + 1]
            after[i] = term if i == cells_x - 2 else after[i + 1] + term
        for i in range(cells_x):
            total = at_x(4, i) * stations[i]
            if i > 0:
                total = total + at_x(0, i) * before[i] + at_x(5, i) * stations[i - 1]
            if i < cells_x - 1:
                total = total + at_x(1, i) * after[i] + at_x(6, i) * stations[i + 1]

            line = flux_y[f, i]
            below = wide[2] * line
            above = wide[3] * line
            low = jnp.where(station >= 1, pltpu.roll(line, 1, 0), 0.0)
            high = jnp.where(station < cells_y - 1, pltpu.roll(line, cells_y - 1, 0), 0.0)
            below = jnp.where(station >= 1, pltpu.roll(below, 1, 0), 0.0)
            above = jnp.where(station < cells_y - 1, pltpu.roll(above, cells_y - 1, 0), 0.0)
            step = 1
            while step < cells_y:
                below = below + jnp.where(station >= step, pltpu.roll(below, step, 0), 0.0)
                above = above + jnp.where(
                    station < cells_y - step, pltpu.roll(above, cells_y - step, 0), 0.0
                )
                step *= 2
            total = total + wide[0] * below + wide[1] * above
            total = total + wide[4] * line + wide[5] * low + wide[6] * high
            out[f, i] = total


def far_x_kernel(turns_x, base, coef_x_ref, *refs):
    arrived_x, out = refs[:-1], refs[-1]
    fields, cells_x, cells_y, depth = out.shape
    shape = (cells_y, depth)
    coef_x = coef_x_ref[...]
    place = lax.axis_index("gx")
    sides = [upper_of(place, turn) for turn in turns_x]

    def at_x(row, i):
        return jnp.broadcast_to(coef_x[row : row + 1, i : i + 1], shape)

    for f in range(fields):
        for i in range(cells_x):
            total = base[f, i]
            for turn, upper, face in zip(turns_x, sides, arrived_x):
                spot = f * cells_y
                weight = jnp.where(upper, at_x(0, i), at_x(1, i))
                total = total + weight * face[spot : spot + cells_y]
                if not touches(turn):
                    continue
                size = (turn + 1) // 2
                spot = spot + fields * cells_y
                if i == 0:
                    near = upper & (place % size == 0)
                    total = total + jnp.where(near, at_x(5, i), 0.0) * face[spot : spot + cells_y]
                if i == cells_x - 1:
                    near = jnp.logical_not(upper) & (place % size == size - 1)
                    total = total + jnp.where(near, at_x(6, i), 0.0) * face[spot : spot + cells_y]
            out[f, i] = total


def place_kernel(capacity, received, out):
    fields, cells_x, cells_y, depth = out.shape
    rows_block = cells_x * cells_y
    got = jnp.concatenate([received[sender] for sender in range(received.shape[0])], axis=0)
    slots = got.shape[0] * capacity
    flat = [flat_slots(got, f, capacity) for f in range(fields + 1)]
    cell = flat[fields].astype(jnp.int32)
    row_hot = lax.broadcasted_iota(jnp.int32, (rows_block, slots), 0) == cell // depth
    depth_hot = jnp.where(
        lax.broadcasted_iota(jnp.int32, (depth, slots), 0) == cell % depth, 1.0, 0.0
    ).astype(BF16)
    halves = []
    for f in range(fields):
        spread = jnp.where(row_hot, flat[f], 0.0)
        top = spread.astype(BF16)
        halves += [top, (spread - top.astype(F32)).astype(BF16)]
    both = lax.dot_general(
        jnp.concatenate(halves, axis=0), depth_hot, NT, preferred_element_type=F32
    )
    for f in range(fields):
        top = both[2 * f * rows_block : (2 * f + 1) * rows_block]
        forcing = top + both[(2 * f + 1) * rows_block : (2 * f + 2) * rows_block]
        for i in range(cells_x):
            out[f, i] = forcing[i * cells_y : (i + 1) * cells_y]


def last_kernel(turns_z, forcing, base, pair, coef_y_ref, *refs):
    arrived_z, out = refs[:-3], refs[-3]
    held, sems = refs[-2:]
    fields, cells_x, cells_y, depth = out.shape
    shape = (cells_y, depth)
    chip = lax.axis_index("gy") // 2
    odd = lax.axis_index("gy") % 2 == 1

    entering = jnp.where(odd, pair[0], 0.0)
    leaving = jnp.where(odd, 0.0, pair[1])
    left = jnp.where(odd, pair[3], 0.0)
    right = jnp.where(odd, 0.0, pair[2])
    for turn, got in zip(turns_z, arrived_z):
        upper = upper_of(chip, turn)
        entering = entering + jnp.where(upper, got[0], 0.0)
        leaving = leaving + jnp.where(upper, 0.0, got[0])
        if touches(turn):
            size = (turn + 1) // 2
            first = jnp.logical_not(odd) & upper & (chip % size == 0)
            last = odd & jnp.logical_not(upper) & (chip % size == size - 1)
            left = jnp.where(first, got[1], left)
            right = jnp.where(last, got[1], right)

    coef_y = coef_y_ref[...]

    p_y = jnp.broadcast_to(coef_y[:, 0:1], shape)
    u_y = jnp.broadcast_to(coef_y[:, 1:2], shape)
    station = lax.broadcasted_iota(jnp.int32, shape, 0)
    low_y = jnp.where(station == 0, jnp.broadcast_to(coef_y[:, 5:6], shape), 0.0)
    high_y = jnp.where(station == cells_y - 1, jnp.broadcast_to(coef_y[:, 6:7], shape), 0.0)
    copies = []
    for f in range(fields):
        for i in range(cells_x):
            total = base[f, i]
            line = slice(f * cells_x + i, f * cells_x + i + 1)
            total = total + p_y * entering[line] + u_y * leaving[line]
            total = total + low_y * left[line] + high_y * right[line]
            held[f, i] = forcing[f, i] - total
        copies.append(pltpu.make_async_copy(held.at[f], out.at[f], sems.at[f]))
        copies[-1].start()
    for copy in copies:
        copy.wait()


def along_z(own, pair, turns):
    count = lax.axis_size("gy")
    place = lax.axis_index("gy")
    odd = place % 2 == 1
    sum_t, sum_u = own[0] + pair[0], own[1] + pair[1]
    first, last = jnp.where(odd, pair[2], own[2]), jnp.where(odd, own[3], pair[3])
    sent = {}
    for turn in turns:
        bit = turn.bit_length()
        if bit not in sent:
            upper = upper_of(place // 2, turn)
            sent[bit] = jnp.stack([jnp.where(upper, sum_u, sum_t), jnp.where(upper, first, last)])
    return [
        lax.ppermute(sent[turn.bit_length()], "gy", [(i, i ^ (2 * turn + 1)) for i in range(count)])
        for turn in turns
    ]


def on_device(
    adjoint, jac_x, jac_y, alpha_x, metric_x, alpha_y, metric_y, surf_values, surf_cells, surf_owner
):
    fields, cells_x, cells_y, depth = adjoint.shape
    points = surf_values.shape[2]
    n_x = lax.axis_size("gx")
    n_y = lax.axis_size("gy")
    devices = n_x * n_y
    capacity = max(4, 2 * points // devices)
    sizes = (alpha_x.shape[0], alpha_y.shape[0])
    lanes = -(-max(sizes) // 128) * 128
    lines = fields * cells_x
    vmem = pl.BlockSpec(memory_space=pltpu.VMEM)
    hbm = pl.BlockSpec(memory_space=pltpu.HBM)

    def array(*shape):
        return jax.ShapeDtypeStruct(shape, F32)

    def cost(micros):
        return pl.CostEstimate(
            flops=int(micros * 1e9), bytes_accessed=int(micros * 3.6e6), transcendentals=0
        )

    params = pltpu.CompilerParams(vmem_limit_bytes=24 << 20)
    inputs = [
        alpha_x.reshape(1, -1),
        alpha_y.reshape(1, -1),
        metric_x.reshape(1, -1),
        metric_y.reshape(1, -1),
        jnp.transpose(surf_values, (1, 0, 2)),
        surf_cells,
        surf_owner.reshape(1, points),
        adjoint,
        jac_x,
        jac_y,
    ]
    turns_x = tuple(range(n_x - 1, 0, -1))
    turns_z = tuple(range(1, n_y // 2))
    width = -(-(fields + 1) * capacity // 128) * 128
    face_rows = fields * cells_y
    flux_x, flux_y, own_y, coef_x, coef_y, pack, *faces = pl.pallas_call(
        functools.partial(first_kernel, sizes, capacity, turns_x),
        in_specs=[hbm] * len(inputs),
        out_specs=[vmem] * 5 + [pl.BlockSpec(memory_space=pl.ANY)] + [vmem] * len(turns_x),
        out_shape=[
            array(*adjoint.shape),
            array(*adjoint.shape),
            array(4, lines, depth),
            array(8, 128),
            array(cells_y, 128),
            array(devices, 1, width),
        ]
        + [array((2 if touches(turn) else 1) * face_rows, depth) for turn in turns_x],
        scratch_shapes=[pltpu.VMEM(a.shape, a.dtype) for a in inputs]
        + [
            pltpu.VMEM((8, lanes), F32),
            pltpu.VMEM((devices, 1, width), F32),
            pltpu.SemaphoreType.DMA((len(inputs) + 1,)),
        ],
        compiler_params=params,
        cost_estimate=cost(2.5),
        name="flux_and_sums",
    )(*[pltpu.with_memory_space_constraint(a, pltpu.HBM) for a in inputs])
    received = lax.all_to_all(pack, ("gx", "gy"), 0, 0, tiled=True)
    arrived = {}
    for turn, face in sorted(zip(turns_x, faces), key=lambda item: not touches(item[0])):
        if not touches(turn):
            face, arrived[n_x - 1] = lax.optimization_barrier((face, arrived[n_x - 1]))
        arrived[turn] = lax.ppermute(face, "gx", [(i, i ^ turn) for i in range(n_x)])
    arrived_x = [arrived[turn] for turn in turns_x]
    pair = lax.ppermute(own_y, "gy", [(i, i ^ 1) for i in range(n_y)])
    arrived_z = along_z(own_y, pair, turns_z)
    base = pl.pallas_call(
        block_kernel,
        in_specs=[vmem] * 4,
        out_specs=vmem,
        out_shape=array(*adjoint.shape),
        compiler_params=params,
        cost_estimate=cost(5),
        name="block_part",
    )(flux_x, flux_y, coef_x, coef_y)
    base = pl.pallas_call(
        functools.partial(far_x_kernel, turns_x),
        in_specs=[vmem] * (2 + len(turns_x)),
        out_specs=vmem,
        out_shape=array(*adjoint.shape),
        compiler_params=params,
        cost_estimate=cost(0.33),
        name="far_x_part",
    )(base, coef_x, *arrived_x)
    forcing = pl.pallas_call(
        functools.partial(place_kernel, capacity),
        in_specs=[vmem],
        out_specs=vmem,
        out_shape=array(*adjoint.shape),
        compiler_params=params,
        cost_estimate=cost(0.01),
        name="placed_points",
    )(received)
    return pl.pallas_call(
        functools.partial(last_kernel, turns_z),
        in_specs=[vmem] * (4 + len(turns_z)),
        out_specs=pl.BlockSpec(memory_space=pl.ANY),
        out_shape=array(*adjoint.shape),
        scratch_shapes=[
            pltpu.VMEM(adjoint.shape, F32),
            pltpu.SemaphoreType.DMA((fields,)),
        ],
        compiler_params=params,
        cost_estimate=cost(1),
        name="far_part",
    )(forcing, base, pair, coef_y, *arrived_z)


def solution(mesh):
    in_specs = (
        P(None, "gx", "gy", None),
        P(None, None, "gx", "gy", None),
        P(None, None, "gx", "gy", None),
        P(),
        P("gx"),
        P(),
        P("gy"),
        P(("gx", "gy"), None, None),
        P(("gx", "gy"), None),
        P(("gx", "gy"), None, None),
    )
    out_specs = P(None, "gx", "gy", None)
    return jax.shard_map(
        on_device, mesh=mesh, in_specs=in_specs, out_specs=out_specs, check_vma=False
    )
```

```python
import functools

import jax
import jax.numpy as jnp
from jax import lax
from jax.experimental import pallas as pl
from jax.experimental.pallas import tpu as pltpu
from jax.sharding import PartitionSpec as P

F32 = jnp.float32
BF16 = jnp.bfloat16
NT = (((1,), (1,)), ((), ()))


def moved(row, by, lane, fill):
    lanes = row.shape[1]
    turned = pltpu.roll(row, by % lanes, 1)
    keep = (lane >= by) if by > 0 else (lane < lanes + by)
    return jnp.where(keep, turned, fill)


def running(parts, lane, direction):
    lanes = lane.shape[1]
    a, b, c, d = parts
    step = 1
    while step < lanes:
        shift = step * direction
        a0, b0 = moved(a, shift, lane, 1.0), moved(b, shift, lane, 0.0)
        c0, d0 = moved(c, shift, lane, 0.0), moved(d, shift, lane, 1.0)
        a, b, c, d = a * a0 + b * c0, a * b0 + b * d0, c * a0 + d * c0, c * b0 + d * d0
        step *= 2
    return a + b


def line_rows(alpha, sizes):
    axes, lanes = alpha.shape
    lane = lax.broadcasted_iota(jnp.int32, (axes, lanes), 1)
    which = lax.broadcasted_iota(jnp.int32, (axes, lanes), 0)
    count = jnp.zeros((axes, lanes), jnp.int32)
    for axis, size in enumerate(sizes):
        count = jnp.where(which == axis, size, count)
    inside = lane < count
    alpha = jnp.where(inside, alpha, 0.5)
    slack = 1.0 - 2.0 * alpha
    twice = 2.0 * alpha

    eps = slack + twice * moved(slack, 1, lane, 0.0)
    c = 1.0 - eps
    fwd = running((1.0 + eps, c, eps, c), lane, 1)
    eps = slack + twice * moved(slack, -1, lane, 0.0)
    c = 1.0 - eps
    bwd = running(
        (
            jnp.where(inside, 1.0 + eps, 1.0),
            jnp.where(inside, c, 0.0),
            jnp.where(inside, eps, 0.0),
            jnp.where(inside, c, 1.0),
        ),
        lane,
        -1,
    )
    weight = twice
    step = 1
    while step < lanes:
        weight = weight * moved(weight, step, lane, 1.0)
        step *= 2
    before_w = moved(weight, 1, lane, 1.0)
    before_f = moved(fwd, 1, lane, 1.0)
    after_g = moved(bwd, -1, lane, 1.0)
    whole = jnp.sum(jnp.where(lane == count - 1, fwd, 0.0), axis=1, keepdims=True)
    sign = jnp.where(lane % 2 == 0, 1.0, -1.0)

    p = jnp.where(inside, sign * weight * after_g, 0.0)
    u = jnp.where(inside, sign * before_f / before_w, 0.0)
    q = jnp.where(inside, 2.0 * sign * before_f / (weight * whole), 0.0)
    v = jnp.where(inside, 2.0 * sign * before_w * after_g / whole, 0.0)
    near = (alpha + 2.0) / 3.0
    far = (4.0 * alpha - 1.0) / 12.0

    def folded(row):
        one, two = row * near, row * far
        return (
            moved(one, 1, lane, 0.0)
            - moved(one, -1, lane, 0.0)
            + moved(two, 2, lane, 0.0)
            - moved(two, -2, lane, 0.0)
        )

    diag = p * (moved(q * near, 1, lane, 0.0) + moved(q * far, 2, lane, 0.0)) - u * (
        moved(v * near, -1, lane, 0.0) + moved(v * far, -2, lane, 0.0)
    )
    next_far = moved(jnp.where(inside, far, 0.0), -1, lane, 0.0)
    last_far = moved(far, 1, lane, 0.0)
    low = (p * moved(q, -1, lane, 0.0) - u * moved(v, -1, lane, 0.0)) * next_far
    high = (p * moved(q, 1, lane, 0.0) - u * moved(v, 1, lane, 0.0)) * last_far
    t = jnp.where(inside, folded(q), 0.0)
    s = jnp.where(inside, folded(v), 0.0)
    return [p, u, t, s, diag, low, high]


def packed_points(values, cells, owners, devices, capacity, width):
    points = owners.shape[1]
    row = lax.broadcasted_iota(jnp.int32, (devices, points), 0)
    hot = jnp.where(row == owners, 1.0, 0.0)
    group = 128
    upper = jnp.where(
        lax.broadcasted_iota(jnp.int32, (group, group), 0)
        < lax.broadcasted_iota(jnp.int32, (group, group), 1),
        1.0,
        0.0,
    ).astype(BF16)
    carried = jnp.zeros((devices, 1), F32)
    ranks = []
    for start in range(0, points, group):
        piece = hot[:, start : start + group]
        counts = carried + jnp.dot(piece.astype(BF16), upper, preferred_element_type=F32)
        ranks.append(jnp.sum(piece * counts, axis=0, keepdims=True))
        carried = carried + jnp.sum(piece, axis=1, keepdims=True)
    rank = jnp.concatenate(ranks, axis=1).astype(jnp.int32)
    slot = lax.broadcasted_iota(jnp.int32, (capacity, points), 0) == rank
    rows = [jnp.where(slot, row, 0.0) for row in values]
    rows.append(jnp.where(slot, cells.astype(F32), 0.0))
    spread = jnp.concatenate(rows, axis=0)
    top = spread.astype(BF16)
    rest = (spread - top.astype(F32)).astype(BF16)
    hot = hot.astype(BF16)
    spare = width - spread.shape[0]
    if spare:
        top = jnp.concatenate([top, jnp.zeros((spare, points), BF16)], axis=0)
        rest = jnp.concatenate([rest, jnp.zeros((spare, points), BF16)], axis=0)
    return lax.dot_general(hot, top, NT, preferred_element_type=F32) + lax.dot_general(
        hot, rest, NT, preferred_element_type=F32
    )


def fetch(sources, targets, sems):
    copies = [
        pltpu.make_async_copy(source, target, sems.at[number])
        for number, (source, target) in enumerate(zip(sources, targets))
    ]
    for copy in copies:
        copy.start()
    return copies


def first_kernel(sizes, capacity, turns, *refs):
    sources, refs = refs[:10], refs[10:]
    flux_x_out, flux_y_out, send_y, coef_x_out, coef_y_out, pack_out = refs[:6]
    faces, targets, alpha_s, pack, sems = refs[6:-13], refs[-13:-3], refs[-3], refs[-2], refs[-1]
    alpha_x, alpha_y, metric_x, metric_y, values, cells, owners, adj, jx, jy = targets
    copies = fetch(sources, targets, sems)
    for copy in copies[:7]:
        copy.wait()
    fields, cells_x, cells_y, depth = adj.shape
    lanes = alpha_s.shape[1]
    place_x = lax.axis_index("gx")
    shape = (cells_y, depth)

    devices, _, width = pack.shape
    packed = packed_points(
        [values[f] for f in range(fields)], cells[...], owners[...], devices, capacity, width
    )
    for device in range(devices):
        pack[device] = packed[device : device + 1]
    leaving = pltpu.make_async_copy(pack, pack_out, sems.at[len(sources)])
    leaving.start()

    alpha_s[...] = jnp.full(alpha_s.shape, 0.5, F32)
    alpha_s[0:1, 0 : sizes[0]] = alpha_x[...]
    alpha_s[1:2, 0 : sizes[1]] = alpha_y[...]
    rows = line_rows(alpha_s[...], sizes)
    first_x = place_x * cells_x
    first_y = lax.axis_index("gy") * cells_y
    coef_x = jnp.concatenate([row[0:1] for row in rows] + [jnp.zeros((1, lanes), F32)], axis=0)
    coef_y = jnp.concatenate([row[1:2] for row in rows] + [jnp.zeros((1, lanes), F32)], axis=0)
    coef_x = pltpu.roll(coef_x, lax.rem(lanes - first_x, lanes), 1)[:, :128]
    coef_y = pltpu.roll(coef_y, lax.rem(lanes - first_y, lanes), 1)[:, :128]
    row_of = lax.broadcasted_iota(jnp.int32, (8, 128), 0)
    scaled = (row_of != 2) & (row_of != 3)
    gain_x = jnp.concatenate([metric_x[...], jnp.zeros((1, 128 - cells_x), F32)], axis=1)
    gain_y = jnp.concatenate([metric_y[...], jnp.zeros((1, 128 - cells_y), F32)], axis=1)
    coef_x = coef_x * jnp.where(scaled, gain_x, 1.0)
    coef_y = coef_y * jnp.where(scaled, gain_y, 1.0)
    coef_x_out[...] = coef_x
    columns_y = jnp.concatenate([coef_y, jnp.zeros((120, 128), F32)], axis=0).T[:cells_y]
    coef_y_out[...] = columns_y

    copies[7].wait()
    copies[8].wait()
    totals = [[None, None] for _ in range(fields)]
    for i in range(cells_x):
        state = [adj[k, i] for k in range(fields)]
        for target in range(fields):
            flux = jx[0, target, i].astype(F32) * state[0]
            for k in range(1, fields):
                flux = flux + jx[k, target, i].astype(F32) * state[k]
            flux_x_out[target, i] = flux
            for side in range(2):
                term = jnp.broadcast_to(coef_x[2 + side : 3 + side, i : i + 1], shape) * flux
                if i > 0:
                    term = totals[target][side] + term
                totals[target][side] = term
    for turn, face in zip(turns, faces):
        size = 1 << (turn.bit_length() - 1)
        upper = (place_x // size) % 2 == 1
        for target in range(fields):
            spot = target * cells_y
            face[spot : spot + cells_y] = jnp.where(upper, totals[target][1], totals[target][0])
            if touches(turn):
                spot = spot + fields * cells_y
                face[spot : spot + cells_y] = jnp.where(
                    upper, flux_x_out[target, 0], flux_x_out[target, cells_x - 1]
                )

    weight_t = jnp.broadcast_to(columns_y[:, 2:3], shape)
    weight_s = jnp.broadcast_to(columns_y[:, 3:4], shape)
    copies[9].wait()
    for i in range(cells_x):
        state = [adj[k, i] for k in range(fields)]
        for target in range(fields):
            flux = jy[0, target, i].astype(F32) * state[0]
            for k in range(1, fields):
                flux = flux + jy[k, target, i].astype(F32) * state[k]
            flux_y_out[target, i] = flux
            line = target * cells_x + i
            rows = (
                jnp.sum(weight_t * flux, axis=0, keepdims=True),
                jnp.sum(weight_s * flux, axis=0, keepdims=True),
                flux[0:1],
                flux[cells_y - 1 : cells_y],
            )
            for number, row in enumerate(rows):
                send_y[number, line : line + 1] = row
    leaving.wait()


def flat_slots(received, number, capacity):
    senders = received.shape[0]
    part = received[:, number * capacity : (number + 1) * capacity]
    repeats = 128 // capacity
    tiled = jnp.concatenate([part] * repeats, axis=1)
    lane = lax.broadcasted_iota(jnp.int32, (senders, 128), 1) // capacity
    sender = lax.broadcasted_iota(jnp.int32, (senders, 128), 0)
    rows = []
    for group in range(senders // repeats):
        mine = sender == lane + group * repeats
        rows.append(jnp.sum(jnp.where(mine, tiled, 0.0), axis=0, keepdims=True))
    return jnp.concatenate(rows, axis=1)


def touches(turn):
    return turn & (turn + 1) == 0


def upper_of(place, turn):
    return (place // (1 << (turn.bit_length() - 1))) % 2 == 1


def block_kernel(flux_x, flux_y, coef_x_ref, coef_y_ref, out):
    fields, cells_x, cells_y, depth = out.shape
    shape = (cells_y, depth)
    coef_x = coef_x_ref[...]
    coef_y = coef_y_ref[...]

    def at_x(row, i):
        return jnp.broadcast_to(coef_x[row : row + 1, i : i + 1], shape)

    wide = [jnp.broadcast_to(coef_y[:, row : row + 1], shape) for row in range(7)]
    station = lax.broadcasted_iota(jnp.int32, shape, 0)

    for f in range(fields):
        stations = [flux_x[f, i] for i in range(cells_x)]
        before = [None] * cells_x
        after = [None] * cells_x
        for i in range(1, cells_x):
            term = at_x(2, i - 1) * stations[i - 1]
            before[i] = term if i == 1 else before[i - 1] + term
        for i in range(cells_x - 2, -1, -1):
            term = at_x(3, i + 1) * stations[i + 1]
            after[i] = term if i == cells_x - 2 else after[i + 1] + term
        for i in range(cells_x):
            total = at_x(4, i) * stations[i]
            if i > 0:
                total = total + at_x(0, i) * before[i] + at_x(5, i) * stations[i - 1]
            if i < cells_x - 1:
                total = total + at_x(1, i) * after[i] + at_x(6, i) * stations[i + 1]

            line = flux_y[f, i]
            below = wide[2] * line
            above = wide[3] * line
            low = jnp.where(station >= 1, pltpu.roll(line, 1, 0), 0.0)
            high = jnp.where(station < cells_y - 1, pltpu.roll(line, cells_y - 1, 0), 0.0)
            below = jnp.where(station >= 1, pltpu.roll(below, 1, 0), 0.0)
            above = jnp.where(station < cells_y - 1, pltpu.roll(above, cells_y - 1, 0), 0.0)
            step = 1
            while step < cells_y:
                below = below + jnp.where(station >= step, pltpu.roll(below, step, 0), 0.0)
                above = above + jnp.where(
                    station < cells_y - step, pltpu.roll(above, cells_y - step, 0), 0.0
                )
                step *= 2
            total = total + wide[0] * below + wide[1] * above
            total = total + wide[4] * line + wide[5] * low + wide[6] * high
            out[f, i] = total


def far_x_kernel(turns_x, base, coef_x_ref, *refs):
    arrived_x, out = refs[:-1], refs[-1]
    fields, cells_x, cells_y, depth = out.shape
    shape = (cells_y, depth)
    coef_x = coef_x_ref[...]
    place = lax.axis_index("gx")
    sides = [upper_of(place, turn) for turn in turns_x]

    def at_x(row, i):
        return jnp.broadcast_to(coef_x[row : row + 1, i : i + 1], shape)

    for f in range(fields):
        for i in range(cells_x):
            total = base[f, i]
            for turn, upper, face in zip(turns_x, sides, arrived_x):
                spot = f * cells_y
                weight = jnp.where(upper, at_x(0, i), at_x(1, i))
                total = total + weight * face[spot : spot + cells_y]
                if not touches(turn):
                    continue
                size = (turn + 1) // 2
                spot = spot + fields * cells_y
                if i == 0:
                    near = upper & (place % size == 0)
                    total = total + jnp.where(near, at_x(5, i), 0.0) * face[spot : spot + cells_y]
                if i == cells_x - 1:
                    near = jnp.logical_not(upper) & (place % size == size - 1)
                    total = total + jnp.where(near, at_x(6, i), 0.0) * face[spot : spot + cells_y]
            out[f, i] = total


def place_kernel(capacity, received, out):
    fields, cells_x, cells_y, depth = out.shape
    rows_block = cells_x * cells_y
    got = jnp.concatenate([received[sender] for sender in range(received.shape[0])], axis=0)
    slots = got.shape[0] * capacity
    flat = [flat_slots(got, f, capacity) for f in range(fields + 1)]
    cell = flat[fields].astype(jnp.int32)
    row_hot = lax.broadcasted_iota(jnp.int32, (rows_block, slots), 0) == cell // depth
    depth_hot = jnp.where(
        lax.broadcasted_iota(jnp.int32, (depth, slots), 0) == cell % depth, 1.0, 0.0
    ).astype(BF16)
    halves = []
    for f in range(fields):
        spread = jnp.where(row_hot, flat[f], 0.0)
        top = spread.astype(BF16)
        halves += [top, (spread - top.astype(F32)).astype(BF16)]
    both = lax.dot_general(
        jnp.concatenate(halves, axis=0), depth_hot, NT, preferred_element_type=F32
    )
    for f in range(fields):
        top = both[2 * f * rows_block : (2 * f + 1) * rows_block]
        forcing = top + both[(2 * f + 1) * rows_block : (2 * f + 2) * rows_block]
        for i in range(cells_x):
            out[f, i] = forcing[i * cells_y : (i + 1) * cells_y]


def last_kernel(turns_z, forcing, base, pair, coef_y_ref, *refs):
    arrived_z, out = refs[:-3], refs[-3]
    held, sems = refs[-2:]
    fields, cells_x, cells_y, depth = out.shape
    shape = (cells_y, depth)
    chip = lax.axis_index("gy") // 2
    odd = lax.axis_index("gy") % 2 == 1

    entering = jnp.where(odd, pair[0], 0.0)
    leaving = jnp.where(odd, 0.0, pair[1])
    left = jnp.where(odd, pair[3], 0.0)
    right = jnp.where(odd, 0.0, pair[2])
    for turn, got in zip(turns_z, arrived_z):
        upper = upper_of(chip, turn)
        entering = entering + jnp.where(upper, got[0], 0.0)
        leaving = leaving + jnp.where(upper, 0.0, got[0])
        if touches(turn):
            size = (turn + 1) // 2
            first = jnp.logical_not(odd) & upper & (chip % size == 0)
            last = odd & jnp.logical_not(upper) & (chip % size == size - 1)
            left = jnp.where(first, got[1], left)
            right = jnp.where(last, got[1], right)

    coef_y = coef_y_ref[...]

    p_y = jnp.broadcast_to(coef_y[:, 0:1], shape)
    u_y = jnp.broadcast_to(coef_y[:, 1:2], shape)
    station = lax.broadcasted_iota(jnp.int32, shape, 0)
    low_y = jnp.where(station == 0, jnp.broadcast_to(coef_y[:, 5:6], shape), 0.0)
    high_y = jnp.where(station == cells_y - 1, jnp.broadcast_to(coef_y[:, 6:7], shape), 0.0)
    copies = []
    for f in range(fields):
        for i in range(cells_x):
            total = base[f, i]
            line = slice(f * cells_x + i, f * cells_x + i + 1)
            total = total + p_y * entering[line] + u_y * leaving[line]
            total = total + low_y * left[line] + high_y * right[line]
            held[f, i] = forcing[f, i] - total
        copies.append(pltpu.make_async_copy(held.at[f], out.at[f], sems.at[f]))
        copies[-1].start()
    for copy in copies:
        copy.wait()


def along_z(own, pair, turns):
    count = lax.axis_size("gy")
    place = lax.axis_index("gy")
    odd = place % 2 == 1
    sum_t, sum_u = own[0] + pair[0], own[1] + pair[1]
    first, last = jnp.where(odd, pair[2], own[2]), jnp.where(odd, own[3], pair[3])
    sent = {}
    for turn in turns:
        bit = turn.bit_length()
        if bit not in sent:
            upper = upper_of(place // 2, turn)
            sent[bit] = jnp.stack([jnp.where(upper, sum_u, sum_t), jnp.where(upper, first, last)])
    return [
        lax.ppermute(sent[turn.bit_length()], "gy", [(i, i ^ (2 * turn + 1)) for i in range(count)])
        for turn in turns
    ]


def on_device(
    adjoint, jac_x, jac_y, alpha_x, metric_x, alpha_y, metric_y, surf_values, surf_cells, surf_owner
):
    fields, cells_x, cells_y, depth = adjoint.shape
    points = surf_values.shape[2]
    n_x = lax.axis_size("gx")
    n_y = lax.axis_size("gy")
    devices = n_x * n_y
    capacity = max(4, 2 * points // devices)
    sizes = (alpha_x.shape[0], alpha_y.shape[0])
    lanes = -(-max(sizes) // 128) * 128
    lines = fields * cells_x
    vmem = pl.BlockSpec(memory_space=pltpu.VMEM)
    hbm = pl.BlockSpec(memory_space=pltpu.HBM)

    def array(*shape):
        return jax.ShapeDtypeStruct(shape, F32)

    def cost(micros):
        return pl.CostEstimate(
            flops=int(micros * 1e9), bytes_accessed=int(micros * 3.6e6), transcendentals=0
        )

    params = pltpu.CompilerParams(vmem_limit_bytes=24 << 20)
    inputs = [
        alpha_x.reshape(1, -1),
        alpha_y.reshape(1, -1),
        metric_x.reshape(1, -1),
        metric_y.reshape(1, -1),
        jnp.transpose(surf_values, (1, 0, 2)),
        surf_cells,
        surf_owner.reshape(1, points),
        adjoint,
        jac_x,
        jac_y,
    ]
    turns_x = tuple(range(n_x - 1, 0, -1))
    turns_z = tuple(range(1, n_y // 2))
    width = -(-(fields + 1) * capacity // 128) * 128
    face_rows = fields * cells_y
    flux_x, flux_y, own_y, coef_x, coef_y, pack, *faces = pl.pallas_call(
        functools.partial(first_kernel, sizes, capacity, turns_x),
        in_specs=[hbm] * len(inputs),
        out_specs=[vmem] * 5 + [pl.BlockSpec(memory_space=pl.ANY)] + [vmem] * len(turns_x),
        out_shape=[
            array(*adjoint.shape),
            array(*adjoint.shape),
            array(4, lines, depth),
            array(8, 128),
            array(cells_y, 128),
            array(devices, 1, width),
        ]
        + [array((2 if touches(turn) else 1) * face_rows, depth) for turn in turns_x],
        scratch_shapes=[pltpu.VMEM(a.shape, a.dtype) for a in inputs]
        + [
            pltpu.VMEM((8, lanes), F32),
            pltpu.VMEM((devices, 1, width), F32),
            pltpu.SemaphoreType.DMA((len(inputs) + 1,)),
        ],
        compiler_params=params,
        cost_estimate=cost(2.5),
        name="flux_and_sums",
    )(*[pltpu.with_memory_space_constraint(a, pltpu.HBM) for a in inputs])
    received = lax.all_to_all(pack, ("gx", "gy"), 0, 0, tiled=True)
    arrived = {}
    for turn, face in sorted(zip(turns_x, faces), key=lambda item: not touches(item[0])):
        if not touches(turn):
            face, arrived[n_x - 1] = lax.optimization_barrier((face, arrived[n_x - 1]))
        arrived[turn] = lax.ppermute(face, "gx", [(i, i ^ turn) for i in range(n_x)])
    arrived_x = [arrived[turn] for turn in turns_x]
    pair = lax.ppermute(own_y, "gy", [(i, i ^ 1) for i in range(n_y)])
    arrived_z = along_z(own_y, pair, turns_z)
    base = pl.pallas_call(
        block_kernel,
        in_specs=[vmem] * 4,
        out_specs=vmem,
        out_shape=array(*adjoint.shape),
        compiler_params=params,
        cost_estimate=cost(5),
        name="block_part",
    )(flux_x, flux_y, coef_x, coef_y)
    base = pl.pallas_call(
        functools.partial(far_x_kernel, turns_x),
        in_specs=[vmem] * (2 + len(turns_x)),
        out_specs=vmem,
        out_shape=array(*adjoint.shape),
        compiler_params=params,
        cost_estimate=cost(0.33),
        name="far_x_part",
    )(base, coef_x, *arrived_x)
    forcing = pl.pallas_call(
        functools.partial(place_kernel, capacity),
        in_specs=[vmem],
        out_specs=vmem,
        out_shape=array(*adjoint.shape),
        compiler_params=params,
        cost_estimate=cost(0.01),
        name="placed_points",
    )(received)
    return pl.pallas_call(
        functools.partial(last_kernel, turns_z),
        in_specs=[vmem] * (4 + len(turns_z)),
        out_specs=pl.BlockSpec(memory_space=pl.ANY),
        out_shape=array(*adjoint.shape),
        scratch_shapes=[
            pltpu.VMEM(adjoint.shape, F32),
            pltpu.SemaphoreType.DMA((fields,)),
        ],
        compiler_params=params,
        cost_estimate=cost(1),
        name="far_part",
    )(forcing, base, pair, coef_y, *arrived_z)


def solution(mesh):
    in_specs = (
        P(None, "gx", "gy", None),
        P(None, None, "gx", "gy", None),
        P(None, None, "gx", "gy", None),
        P(),
        P("gx"),
        P(),
        P("gy"),
        P(("gx", "gy"), None, None),
        P(("gx", "gy"), None),
        P(("gx", "gy"), None, None),
    )
    out_specs = P(None, "gx", "gy", None)
    return jax.shard_map(
        on_device, mesh=mesh, in_specs=in_specs, out_specs=out_specs, check_vma=False
    )
```

```python
import functools

import jax
import jax.numpy as jnp
from jax import lax
from jax.experimental import pallas as pl
from jax.experimental.pallas import tpu as pltpu
from jax.sharding import PartitionSpec as P

F32 = jnp.float32
BF16 = jnp.bfloat16
NT = (((1,), (1,)), ((), ()))


def moved(row, by, lane, fill):
    lanes = row.shape[1]
    turned = pltpu.roll(row, by % lanes, 1)
    keep = (lane >= by) if by > 0 else (lane < lanes + by)
    return jnp.where(keep, turned, fill)


def running(parts, lane, direction):
    lanes = lane.shape[1]
    a, b, c, d = parts
    step = 1
    while step < lanes:
        shift = step * direction
        a0, b0 = moved(a, shift, lane, 1.0), moved(b, shift, lane, 0.0)
        c0, d0 = moved(c, shift, lane, 0.0), moved(d, shift, lane, 1.0)
        a, b, c, d = a * a0 + b * c0, a * b0 + b * d0, c * a0 + d * c0, c * b0 + d * d0
        step *= 2
    return a + b


def line_rows(alpha, sizes):
    axes, lanes = alpha.shape
    lane = lax.broadcasted_iota(jnp.int32, (axes, lanes), 1)
    which = lax.broadcasted_iota(jnp.int32, (axes, lanes), 0)
    count = jnp.zeros((axes, lanes), jnp.int32)
    for axis, size in enumerate(sizes):
        count = jnp.where(which == axis, size, count)
    inside = lane < count
    alpha = jnp.where(inside, alpha, 0.5)
    slack = 1.0 - 2.0 * alpha
    twice = 2.0 * alpha

    eps = slack + twice * moved(slack, 1, lane, 0.0)
    c = 1.0 - eps
    fwd = running((1.0 + eps, c, eps, c), lane, 1)
    eps = slack + twice * moved(slack, -1, lane, 0.0)
    c = 1.0 - eps
    bwd = running(
        (
            jnp.where(inside, 1.0 + eps, 1.0),
            jnp.where(inside, c, 0.0),
            jnp.where(inside, eps, 0.0),
            jnp.where(inside, c, 1.0),
        ),
        lane,
        -1,
    )
    weight = twice
    step = 1
    while step < lanes:
        weight = weight * moved(weight, step, lane, 1.0)
        step *= 2
    before_w = moved(weight, 1, lane, 1.0)
    before_f = moved(fwd, 1, lane, 1.0)
    after_g = moved(bwd, -1, lane, 1.0)
    whole = jnp.sum(jnp.where(lane == count - 1, fwd, 0.0), axis=1, keepdims=True)
    sign = jnp.where(lane % 2 == 0, 1.0, -1.0)

    p = jnp.where(inside, sign * weight * after_g, 0.0)
    u = jnp.where(inside, sign * before_f / before_w, 0.0)
    q = jnp.where(inside, 2.0 * sign * before_f / (weight * whole), 0.0)
    v = jnp.where(inside, 2.0 * sign * before_w * after_g / whole, 0.0)
    near = (alpha + 2.0) / 3.0
    far = (4.0 * alpha - 1.0) / 12.0

    def folded(row):
        one, two = row * near, row * far
        return (
            moved(one, 1, lane, 0.0)
            - moved(one, -1, lane, 0.0)
            + moved(two, 2, lane, 0.0)
            - moved(two, -2, lane, 0.0)
        )

    diag = p * (moved(q * near, 1, lane, 0.0) + moved(q * far, 2, lane, 0.0)) - u * (
        moved(v * near, -1, lane, 0.0) + moved(v * far, -2, lane, 0.0)
    )
    next_far = moved(jnp.where(inside, far, 0.0), -1, lane, 0.0)
    last_far = moved(far, 1, lane, 0.0)
    low = (p * moved(q, -1, lane, 0.0) - u * moved(v, -1, lane, 0.0)) * next_far
    high = (p * moved(q, 1, lane, 0.0) - u * moved(v, 1, lane, 0.0)) * last_far
    t = jnp.where(inside, folded(q), 0.0)
    s = jnp.where(inside, folded(v), 0.0)
    return [p, u, t, s, diag, low, high]


def packed_points(values, cells, owners, devices, capacity, width):
    points = owners.shape[1]
    row = lax.broadcasted_iota(jnp.int32, (devices, points), 0)
    hot = jnp.where(row == owners, 1.0, 0.0)
    group = 128
    upper = jnp.where(
        lax.broadcasted_iota(jnp.int32, (group, group), 0)
        < lax.broadcasted_iota(jnp.int32, (group, group), 1),
        1.0,
        0.0,
    ).astype(BF16)
    carried = jnp.zeros((devices, 1), F32)
    ranks = []
    for start in range(0, points, group):
        piece = hot[:, start : start + group]
        counts = carried + jnp.dot(piece.astype(BF16), upper, preferred_element_type=F32)
        ranks.append(jnp.sum(piece * counts, axis=0, keepdims=True))
        carried = carried + jnp.sum(piece, axis=1, keepdims=True)
    rank = jnp.concatenate(ranks, axis=1).astype(jnp.int32)
    slot = lax.broadcasted_iota(jnp.int32, (capacity, points), 0) == rank
    rows = [jnp.where(slot, row, 0.0) for row in values]
    rows.append(jnp.where(slot, cells.astype(F32), 0.0))
    spread = jnp.concatenate(rows, axis=0)
    top = spread.astype(BF16)
    rest = (spread - top.astype(F32)).astype(BF16)
    hot = hot.astype(BF16)
    spare = width - spread.shape[0]
    if spare:
        top = jnp.concatenate([top, jnp.zeros((spare, points), BF16)], axis=0)
        rest = jnp.concatenate([rest, jnp.zeros((spare, points), BF16)], axis=0)
    return lax.dot_general(hot, top, NT, preferred_element_type=F32) + lax.dot_general(
        hot, rest, NT, preferred_element_type=F32
    )


def fetch(sources, targets, sems):
    copies = [
        pltpu.make_async_copy(source, target, sems.at[number])
        for number, (source, target) in enumerate(zip(sources, targets))
    ]
    for copy in copies:
        copy.start()
    return copies


def first_kernel(sizes, capacity, turns, *refs):
    sources, refs = refs[:10], refs[10:]
    flux_x_out, flux_y_out, send_y, coef_x_out, coef_y_out, pack_out = refs[:6]
    faces, targets, alpha_s, pack, sems = refs[6:-13], refs[-13:-3], refs[-3], refs[-2], refs[-1]
    alpha_x, alpha_y, metric_x, metric_y, values, cells, owners, adj, jx, jy = targets
    copies = fetch(sources, targets, sems)
    for copy in copies[:7]:
        copy.wait()
    fields, cells_x, cells_y, depth = adj.shape
    lanes = alpha_s.shape[1]
    place_x = lax.axis_index("gx")
    shape = (cells_y, depth)

    alpha_s[...] = jnp.full(alpha_s.shape, 0.5, F32)
    alpha_s[0:1, 0 : sizes[0]] = alpha_x[...]
    alpha_s[1:2, 0 : sizes[1]] = alpha_y[...]
    rows = line_rows(alpha_s[...], sizes)
    first_x = place_x * cells_x
    first_y = lax.axis_index("gy") * cells_y
    coef_x = jnp.concatenate([row[0:1] for row in rows] + [jnp.zeros((1, lanes), F32)], axis=0)
    coef_y = jnp.concatenate([row[1:2] for row in rows] + [jnp.zeros((1, lanes), F32)], axis=0)
    coef_x = pltpu.roll(coef_x, lax.rem(lanes - first_x, lanes), 1)[:, :128]
    coef_y = pltpu.roll(coef_y, lax.rem(lanes - first_y, lanes), 1)[:, :128]
    row_of = lax.broadcasted_iota(jnp.int32, (8, 128), 0)
    scaled = (row_of != 2) & (row_of != 3)
    gain_x = jnp.concatenate([metric_x[...], jnp.zeros((1, 128 - cells_x), F32)], axis=1)
    gain_y = jnp.concatenate([metric_y[...], jnp.zeros((1, 128 - cells_y), F32)], axis=1)
    coef_x = coef_x * jnp.where(scaled, gain_x, 1.0)
    coef_y = coef_y * jnp.where(scaled, gain_y, 1.0)
    coef_x_out[...] = coef_x
    columns_y = jnp.concatenate([coef_y, jnp.zeros((120, 128), F32)], axis=0).T[:cells_y]
    coef_y_out[...] = columns_y

    devices, _, width = pack.shape
    packed = packed_points(
        [values[f] for f in range(fields)], cells[...], owners[...], devices, capacity, width
    )
    for device in range(devices):
        pack[device] = packed[device : device + 1]
    leaving = pltpu.make_async_copy(pack, pack_out, sems.at[len(sources)])
    leaving.start()

    copies[7].wait()
    copies[8].wait()
    totals = [[None, None] for _ in range(fields)]
    for i in range(cells_x):
        state = [adj[k, i] for k in range(fields)]
        for target in range(fields):
            flux = jx[0, target, i].astype(F32) * state[0]
            for k in range(1, fields):
                flux = flux + jx[k, target, i].astype(F32) * state[k]
            flux_x_out[target, i] = flux
            for side in range(2):
                term = jnp.broadcast_to(coef_x[2 + side : 3 + side, i : i + 1], shape) * flux
                if i > 0:
                    term = totals[target][side] + term
                totals[target][side] = term
    for turn, face in zip(turns, faces):
        size = 1 << (turn.bit_length() - 1)
        upper = (place_x // size) % 2 == 1
        for target in range(fields):
            spot = target * cells_y
            face[spot : spot + cells_y] = jnp.where(upper, totals[target][1], totals[target][0])
            if touches(turn):
                spot = spot + fields * cells_y
                face[spot : spot + cells_y] = jnp.where(
                    upper, flux_x_out[target, 0], flux_x_out[target, cells_x - 1]
                )

    weight_t = jnp.broadcast_to(columns_y[:, 2:3], shape)
    weight_s = jnp.broadcast_to(columns_y[:, 3:4], shape)
    copies[9].wait()
    for i in range(cells_x):
        state = [adj[k, i] for k in range(fields)]
        for target in range(fields):
            flux = jy[0, target, i].astype(F32) * state[0]
            for k in range(1, fields):
                flux = flux + jy[k, target, i].astype(F32) * state[k]
            flux_y_out[target, i] = flux
            line = target * cells_x + i
            rows = (
                jnp.sum(weight_t * flux, axis=0, keepdims=True),
                jnp.sum(weight_s * flux, axis=0, keepdims=True),
                flux[0:1],
                flux[cells_y - 1 : cells_y],
            )
            for number, row in enumerate(rows):
                send_y[number, line : line + 1] = row
    leaving.wait()


def flat_slots(received, number, capacity):
    senders = received.shape[0]
    part = received[:, number * capacity : (number + 1) * capacity]
    repeats = 128 // capacity
    tiled = jnp.concatenate([part] * repeats, axis=1)
    lane = lax.broadcasted_iota(jnp.int32, (senders, 128), 1) // capacity
    sender = lax.broadcasted_iota(jnp.int32, (senders, 128), 0)
    rows = []
    for group in range(senders // repeats):
        mine = sender == lane + group * repeats
        rows.append(jnp.sum(jnp.where(mine, tiled, 0.0), axis=0, keepdims=True))
    return jnp.concatenate(rows, axis=1)


def touches(turn):
    return turn & (turn + 1) == 0


def upper_of(place, turn):
    return (place // (1 << (turn.bit_length() - 1))) % 2 == 1


def block_kernel(flux_x, flux_y, coef_x_ref, coef_y_ref, out):
    fields, cells_x, cells_y, depth = out.shape
    shape = (cells_y, depth)
    coef_x = coef_x_ref[...]
    coef_y = coef_y_ref[...]

    def at_x(row, i):
        return jnp.broadcast_to(coef_x[row : row + 1, i : i + 1], shape)

    wide = [jnp.broadcast_to(coef_y[:, row : row + 1], shape) for row in range(7)]
    station = lax.broadcasted_iota(jnp.int32, shape, 0)

    for f in range(fields):
        stations = [flux_x[f, i] for i in range(cells_x)]
        before = [None] * cells_x
        after = [None] * cells_x
        for i in range(1, cells_x):
            term = at_x(2, i - 1) * stations[i - 1]
            before[i] = term if i == 1 else before[i - 1] + term
        for i in range(cells_x - 2, -1, -1):
            term = at_x(3, i + 1) * stations[i + 1]
            after[i] = term if i == cells_x - 2 else after[i + 1] + term
        for i in range(cells_x):
            total = at_x(4, i) * stations[i]
            if i > 0:
                total = total + at_x(0, i) * before[i] + at_x(5, i) * stations[i - 1]
            if i < cells_x - 1:
                total = total + at_x(1, i) * after[i] + at_x(6, i) * stations[i + 1]

            line = flux_y[f, i]
            below = wide[2] * line
            above = wide[3] * line
            low = jnp.where(station >= 1, pltpu.roll(line, 1, 0), 0.0)
            high = jnp.where(station < cells_y - 1, pltpu.roll(line, cells_y - 1, 0), 0.0)
            below = jnp.where(station >= 1, pltpu.roll(below, 1, 0), 0.0)
            above = jnp.where(station < cells_y - 1, pltpu.roll(above, cells_y - 1, 0), 0.0)
            step = 1
            while step < cells_y:
                below = below + jnp.where(station >= step, pltpu.roll(below, step, 0), 0.0)
                above = above + jnp.where(
                    station < cells_y - step, pltpu.roll(above, cells_y - step, 0), 0.0
                )
                step *= 2
            total = total + wide[0] * below + wide[1] * above
            total = total + wide[4] * line + wide[5] * low + wide[6] * high
            out[f, i] = total


def far_x_kernel(turns_x, base, coef_x_ref, *refs):
    arrived_x, out = refs[:-1], refs[-1]
    fields, cells_x, cells_y, depth = out.shape
    shape = (cells_y, depth)
    coef_x = coef_x_ref[...]
    place = lax.axis_index("gx")
    sides = [upper_of(place, turn) for turn in turns_x]

    def at_x(row, i):
        return jnp.broadcast_to(coef_x[row : row + 1, i : i + 1], shape)

    for f in range(fields):
        for i in range(cells_x):
            total = base[f, i]
            for turn, upper, face in zip(turns_x, sides, arrived_x):
                spot = f * cells_y
                weight = jnp.where(upper, at_x(0, i), at_x(1, i))
                total = total + weight * face[spot : spot + cells_y]
                if not touches(turn):
                    continue
                size = (turn + 1) // 2
                spot = spot + fields * cells_y
                if i == 0:
                    near = upper & (place % size == 0)
                    total = total + jnp.where(near, at_x(5, i), 0.0) * face[spot : spot + cells_y]
                if i == cells_x - 1:
                    near = jnp.logical_not(upper) & (place % size == size - 1)
                    total = total + jnp.where(near, at_x(6, i), 0.0) * face[spot : spot + cells_y]
            out[f, i] = total


def place_kernel(capacity, received, out):
    fields, cells_x, cells_y, depth = out.shape
    rows_block = cells_x * cells_y
    got = jnp.concatenate([received[sender] for sender in range(received.shape[0])], axis=0)
    slots = got.shape[0] * capacity
    flat = [flat_slots(got, f, capacity) for f in range(fields + 1)]
    cell = flat[fields].astype(jnp.int32)
    row_hot = lax.broadcasted_iota(jnp.int32, (rows_block, slots), 0) == cell // depth
    depth_hot = jnp.where(
        lax.broadcasted_iota(jnp.int32, (depth, slots), 0) == cell % depth, 1.0, 0.0
    ).astype(BF16)
    halves = []
    for f in range(fields):
        spread = jnp.where(row_hot, flat[f], 0.0)
        top = spread.astype(BF16)
        halves += [top, (spread - top.astype(F32)).astype(BF16)]
    both = lax.dot_general(
        jnp.concatenate(halves, axis=0), depth_hot, NT, preferred_element_type=F32
    )
    for f in range(fields):
        top = both[2 * f * rows_block : (2 * f + 1) * rows_block]
        forcing = top + both[(2 * f + 1) * rows_block : (2 * f + 2) * rows_block]
        for i in range(cells_x):
            out[f, i] = forcing[i * cells_y : (i + 1) * cells_y]


def last_kernel(turns_z, forcing, base, pair, coef_y_ref, *refs):
    arrived_z, out = refs[:-3], refs[-3]
    held, sems = refs[-2:]
    fields, cells_x, cells_y, depth = out.shape
    shape = (cells_y, depth)
    chip = lax.axis_index("gy") // 2
    odd = lax.axis_index("gy") % 2 == 1

    entering = jnp.where(odd, pair[0], 0.0)
    leaving = jnp.where(odd, 0.0, pair[1])
    left = jnp.where(odd, pair[3], 0.0)
    right = jnp.where(odd, 0.0, pair[2])
    for turn, got in zip(turns_z, arrived_z):
        upper = upper_of(chip, turn)
        entering = entering + jnp.where(upper, got[0], 0.0)
        leaving = leaving + jnp.where(upper, 0.0, got[0])
        if touches(turn):
            size = (turn + 1) // 2
            first = jnp.logical_not(odd) & upper & (chip % size == 0)
            last = odd & jnp.logical_not(upper) & (chip % size == size - 1)
            left = jnp.where(first, got[1], left)
            right = jnp.where(last, got[1], right)

    coef_y = coef_y_ref[...]

    p_y = jnp.broadcast_to(coef_y[:, 0:1], shape)
    u_y = jnp.broadcast_to(coef_y[:, 1:2], shape)
    station = lax.broadcasted_iota(jnp.int32, shape, 0)
    low_y = jnp.where(station == 0, jnp.broadcast_to(coef_y[:, 5:6], shape), 0.0)
    high_y = jnp.where(station == cells_y - 1, jnp.broadcast_to(coef_y[:, 6:7], shape), 0.0)
    copies = []
    for f in range(fields):
        for i in range(cells_x):
            total = base[f, i]
            line = slice(f * cells_x + i, f * cells_x + i + 1)
            total = total + p_y * entering[line] + u_y * leaving[line]
            total = total + low_y * left[line] + high_y * right[line]
            held[f, i] = forcing[f, i] - total
        copies.append(pltpu.make_async_copy(held.at[f], out.at[f], sems.at[f]))
        copies[-1].start()
    for copy in copies:
        copy.wait()


def along_z(own, pair, turns):
    count = lax.axis_size("gy")
    place = lax.axis_index("gy")
    odd = place % 2 == 1
    sum_t, sum_u = own[0] + pair[0], own[1] + pair[1]
    first, last = jnp.where(odd, pair[2], own[2]), jnp.where(odd, own[3], pair[3])
    sent = {}
    for turn in turns:
        bit = turn.bit_length()
        if bit not in sent:
            upper = upper_of(place // 2, turn)
            sent[bit] = jnp.stack([jnp.where(upper, sum_u, sum_t), jnp.where(upper, first, last)])
    return [
        lax.ppermute(sent[turn.bit_length()], "gy", [(i, i ^ (2 * turn + 1)) for i in range(count)])
        for turn in turns
    ]


def on_device(
    adjoint, jac_x, jac_y, alpha_x, metric_x, alpha_y, metric_y, surf_values, surf_cells, surf_owner
):
    fields, cells_x, cells_y, depth = adjoint.shape
    points = surf_values.shape[2]
    n_x = lax.axis_size("gx")
    n_y = lax.axis_size("gy")
    devices = n_x * n_y
    capacity = max(4, 2 * points // devices)
    sizes = (alpha_x.shape[0], alpha_y.shape[0])
    lanes = -(-max(sizes) // 128) * 128
    lines = fields * cells_x
    vmem = pl.BlockSpec(memory_space=pltpu.VMEM)
    hbm = pl.BlockSpec(memory_space=pltpu.HBM)

    def array(*shape):
        return jax.ShapeDtypeStruct(shape, F32)

    def cost(micros):
        return pl.CostEstimate(
            flops=int(micros * 1e9), bytes_accessed=int(micros * 3.6e6), transcendentals=0
        )

    params = pltpu.CompilerParams(vmem_limit_bytes=24 << 20)
    inputs = [
        alpha_x.reshape(1, -1),
        alpha_y.reshape(1, -1),
        metric_x.reshape(1, -1),
        metric_y.reshape(1, -1),
        jnp.transpose(surf_values, (1, 0, 2)),
        surf_cells,
        surf_owner.reshape(1, points),
        adjoint,
        jac_x,
        jac_y,
    ]
    turns_x = tuple(range(n_x - 1, 0, -1))
    turns_z = tuple(sorted(range(1, n_y // 2), key=lambda turn: (touches(turn), turn)))
    width = -(-(fields + 1) * capacity // 128) * 128
    face_rows = fields * cells_y
    flux_x, flux_y, own_y, coef_x, coef_y, pack, *faces = pl.pallas_call(
        functools.partial(first_kernel, sizes, capacity, turns_x),
        in_specs=[hbm] * len(inputs),
        out_specs=[vmem] * 5 + [pl.BlockSpec(memory_space=pl.ANY)] + [vmem] * len(turns_x),
        out_shape=[
            array(*adjoint.shape),
            array(*adjoint.shape),
            array(4, lines, depth),
            array(8, 128),
            array(cells_y, 128),
            array(devices, 1, width),
        ]
        + [array((2 if touches(turn) else 1) * face_rows, depth) for turn in turns_x],
        scratch_shapes=[pltpu.VMEM(a.shape, a.dtype) for a in inputs]
        + [
            pltpu.VMEM((8, lanes), F32),
            pltpu.VMEM((devices, 1, width), F32),
            pltpu.SemaphoreType.DMA((len(inputs) + 1,)),
        ],
        compiler_params=params,
        cost_estimate=cost(2.5),
        name="flux_and_sums",
    )(*[pltpu.with_memory_space_constraint(a, pltpu.HBM) for a in inputs])
    received = lax.all_to_all(pack, ("gx", "gy"), 0, 0, tiled=True)
    arrived = {}
    for turn, face in sorted(zip(turns_x, faces), key=lambda item: not touches(item[0])):
        if not touches(turn):
            face, arrived[n_x - 1] = lax.optimization_barrier((face, arrived[n_x - 1]))
        arrived[turn] = lax.ppermute(face, "gx", [(i, i ^ turn) for i in range(n_x)])
    arrived_x = [arrived[turn] for turn in turns_x]
    pair = lax.ppermute(own_y, "gy", [(i, i ^ 1) for i in range(n_y)])
    arrived_z = along_z(own_y, pair, turns_z)
    base = pl.pallas_call(
        block_kernel,
        in_specs=[vmem] * 4,
        out_specs=vmem,
        out_shape=array(*adjoint.shape),
        compiler_params=params,
        cost_estimate=cost(5),
        name="block_part",
    )(flux_x, flux_y, coef_x, coef_y)
    base = pl.pallas_call(
        functools.partial(far_x_kernel, turns_x),
        in_specs=[vmem] * (2 + len(turns_x)),
        out_specs=vmem,
        out_shape=array(*adjoint.shape),
        compiler_params=params,
        cost_estimate=cost(0.33),
        name="far_x_part",
    )(base, coef_x, *arrived_x)
    forcing = pl.pallas_call(
        functools.partial(place_kernel, capacity),
        in_specs=[vmem],
        out_specs=vmem,
        out_shape=array(*adjoint.shape),
        compiler_params=params,
        cost_estimate=cost(0.01),
        name="placed_points",
    )(received)
    return pl.pallas_call(
        functools.partial(last_kernel, turns_z),
        in_specs=[vmem] * (4 + len(turns_z)),
        out_specs=pl.BlockSpec(memory_space=pl.ANY),
        out_shape=array(*adjoint.shape),
        scratch_shapes=[
            pltpu.VMEM(adjoint.shape, F32),
            pltpu.SemaphoreType.DMA((fields,)),
        ],
        compiler_params=params,
        cost_estimate=cost(1),
        name="far_part",
    )(forcing, base, pair, coef_y, *arrived_z)


def solution(mesh):
    in_specs = (
        P(None, "gx", "gy", None),
        P(None, None, "gx", "gy", None),
        P(None, None, "gx", "gy", None),
        P(),
        P("gx"),
        P(),
        P("gy"),
        P(("gx", "gy"), None, None),
        P(("gx", "gy"), None),
        P(("gx", "gy"), None, None),
    )
    out_specs = P(None, "gx", "gy", None)
    return jax.shard_map(
        on_device, mesh=mesh, in_specs=in_specs, out_specs=out_specs, check_vma=False
    )
```
